128 devices in a mesh: src: 4 (over z), tm: 2 (over core), tile: 16 (over x, y).
Axes of the slice: x: 4, y: 4, z: 4, core: 2. Of those that a mesh axis runs over, the one named last changes fastest.
Arguments:
- latents: bfloat16 [16, 4, 32, 768], P('src', 'tm', 'tile'), may hold values from -6 to 6
- decoder_group: int32 [16, 1], replicated, may hold values from 0 to 3; in each aligned block of 4 rows (0 to 3, 4 to 7, ...) at most 2 rows name the same one
- frames: int32 [16], replicated, may hold values from 1 to 4
- conv_in: bfloat16 [3, 3, 3, 16, 384], replicated, may hold values from -0.3125 to 0.3125
- norm_gain: float32 [384], replicated, may hold values from 0.1 to 1.9
- conv_mid: bfloat16 [3, 3, 3, 384, 384], replicated, may hold values from -0.0625 to 0.0625
- conv_up: bfloat16 [3, 3, 384, 192], replicated, may hold values from -0.109375 to 0.109375
Outputs:
- decoded: bfloat16 [32, 4, 64, 18432], P('src', 'tm', 'tile')
The draws below stay inside these ranges and needn't reach their ends.
Inputs may be any that keep to these rules, and one draw needn't show every extreme that they name: `decoder_group`: among the 4 clips of one sender at most 2 name the same group.
All inputs are finite; a program needn't handle non-finite values.
Results may differ from the reference program's by a relative error of at most 0.009.
Values may be sent and summed in bfloat16 or wider, within the bound.
A program may use at most 128 MiB of HBM per device.

```python
import math
import jax
import jax.numpy as jnp
import numpy as np
from jax import lax

LC = 16
C = 384
C_UP = 192
W = 48
CLIPS = 4
CAP = 2
H = 32
FR = 4
N_SRC = 4


def draw_frames(key, part):
    key = jax.random.fold_in(key, 5)
    counts = jax.random.randint(key, (N_SRC * CLIPS,), 1, FR + 1).astype(jnp.int32)
    return counts.at[0].set(FR)


def block_levels(own_key, extent, split, smallest, high):
    level = 1.0
    for position, parts in split:
        heights = jax.random.uniform(jax.random.fold_in(jax.random.fold_in(own_key, 6), position), (parts,), jnp.float32, smallest / len(split), high / len(split))
        level = level * jnp.repeat(jnp.exp(heights), extent[position] // parts).reshape((-1,) + (1,) * (len(extent) - 1 - position))
    return level


def assign_block(stream_key, own, number, rows, count, top, bound, skew):
    order = jax.random.permutation(stream_key, count)
    heavy_load, usual = portions_of(count, rows * top, bound, skew, True), portions_of(count, rows * top, bound, skew, False)
    places = jnp.arange(count)

    def named(tallies, rotation):
        used = int((tallies > 0).sum())
        fixed = max(1, used // 4)
        shifted = fixed + (places - fixed + rotation * (used - fixed)) % max(1, count - fixed)
        return jnp.zeros((count,), jnp.int32).at[order[jnp.where(places < fixed, places, shifted)]].set(jnp.asarray(tallies, jnp.int32))

    tallies = jnp.where(number % 4 == 0, named(heavy_load, number // 4), named(usual, number - number // 4 - 1))
    mixed = jax.random.permutation(jax.random.fold_in(own, 3), count)
    donor, receiver = mixed[0:count // 2 * 2:2], mixed[1:count // 2 * 2:2]
    slack = jnp.minimum(tallies[donor] - 1, bound - tallies[receiver]) // 2
    slack = jnp.where((donor == order[0]) | (receiver == order[0]) | (tallies[receiver] == 0), 0, jnp.maximum(slack, 0))
    shifted = jax.random.randint(jax.random.fold_in(own, 4), (count // 2,), 0, 1 << 20) % (slack + 1)
    tallies = tallies.at[donor].add(-shifted).at[receiver].add(shifted)
    labels = jnp.searchsorted(jnp.cumsum(tallies), jnp.arange(rows * top), side="right").astype(jnp.int32)
    listing = labels.reshape(top, rows).T
    listing = listing[jax.random.permutation(jax.random.fold_in(own, 1), rows)]
    rotation = jax.random.randint(jax.random.fold_in(own, 2), (rows, 1), 0, top)
    return jnp.take_along_axis(listing, (jnp.arange(top)[None, :] + rotation) % top, axis=1)


def portions_of(number_of, total, reach, slope, full):
    loads = [(1 << 20) // math.isqrt(standing ** slope) + 1 for standing in range(1, number_of + 1)]
    largest = reach if full else min(reach, max(-(-total // number_of), total * loads[0] // sum(loads)))
    least = 1 if total - largest >= number_of - 1 else 0
    given, spare = [largest] + [least] * (number_of - 1), total - largest - least * (number_of - 1)
    while spare > 0:
        candidates = [i for i in range(1, number_of) if given[i] < largest] or [i for i in range(1, number_of) if given[i] < reach]
        whole, remaining = sum([loads[i] for i in candidates]), spare
        for i in candidates:
            extra = min(reach - given[i], max(1, remaining * loads[i] // whole), spare)
            given[i] = given[i] + extra
            spare = spare - extra
    return np.array(given)


def noise(own_key, extent, width, limit, cuts=(), held_as=jnp.bfloat16):
    array = width * jax.random.normal(own_key, extent, jnp.float32)
    if cuts:
        array = array * block_levels(own_key, extent, cuts, -0.22, 0.18)
    return jnp.clip(array, -limit, limit).astype(held_as)


def setup_inputs(seed: int = 0) -> dict:
    seeds = jax.random.split(jax.random.key(seed), 8)
    latents = noise(seeds[0], (N_SRC * CLIPS, FR, H, W * LC), 1.0, 6.0, ((0, 4), (1, 2), (2, 16)))
    decoder_group_keys = jax.random.split(jax.random.fold_in(seeds[1], 1), (N_SRC * CLIPS) // CLIPS)
    decoder_group_turns = jax.random.permutation(jax.random.fold_in(seeds[1], 3), (N_SRC * CLIPS) // CLIPS)
    decoder_group = jax.vmap(lambda own, number: assign_block(jax.random.fold_in(seeds[1], 2), own, number, CLIPS, N_SRC, 1, CAP, 1))(decoder_group_keys, decoder_group_turns).reshape((N_SRC * CLIPS, 1))
    frames = draw_frames(jax.random.fold_in(seeds[7], 71), 0)
    conv_in = noise(seeds[3], (3, 3, 3, LC, C), (27 * LC) ** -0.5, 0.3125)
    norm_gain = jnp.clip(1.0 + 0.18 * jax.random.normal(seeds[4], (C,), jnp.float32), 0.1, 1.9)
    conv_mid = noise(seeds[5], (3, 3, 3, C, C), (27 * C) ** -0.5, 0.0625)
    conv_up = noise(seeds[6], (3, 3, C, C_UP), (9 * C) ** -0.5, 0.109375)
    return dict(latents=latents, decoder_group=decoder_group, frames=frames, conv_in=conv_in, norm_gain=norm_gain, conv_mid=conv_mid, conv_up=conv_up)


def conv_time(padded, kernel):
    return lax.conv_general_dilated(padded.astype(jnp.float32), kernel.astype(jnp.float32), (1, 1, 1), 'VALID', dimension_numbers=('NDHWC', 'DHWIO', 'NDHWC'))

def decode_clip(clip_latent, conv_in, norm_gain, conv_mid, conv_up):
    frame_count, rows, packed = clip_latent.shape
    inputs = clip_latent.reshape(1, frame_count, rows, W, LC)
    spacing = ((0, 0), (2, 0), (1, 1), (1, 1), (0, 0))
    hidden = conv_time(jnp.pad(inputs, spacing), conv_in).astype(jnp.bfloat16)
    hidden_f = hidden.astype(jnp.float32)
    scaled = hidden_f * lax.rsqrt(lax.optimization_barrier(jnp.mean(hidden_f * hidden_f, axis=-1, keepdims=True)) + 1e-06) * norm_gain
    active = jax.nn.silu(scaled).astype(jnp.bfloat16)
    branch = conv_time(jnp.pad(active, spacing), conv_mid)
    residual = (hidden_f + branch).astype(jnp.bfloat16)
    doubled = jnp.repeat(jnp.repeat(residual, 2, axis=2), 2, axis=3)[0]
    doubled = jnp.pad(doubled, ((0, 0), (1, 1), (1, 1), (0, 0)))
    upper = lax.conv_general_dilated(doubled.astype(jnp.float32), conv_up.astype(jnp.float32), (1, 1), 'VALID', dimension_numbers=('NHWC', 'HWIO', 'NHWC'))
    return upper.reshape(frame_count, 2 * rows, 2 * W * C_UP)

def reference(latents, decoder_group, frames, conv_in, norm_gain, conv_mid, conv_up):
    targets = decoder_group[:, 0].reshape(N_SRC, CLIPS)
    same = targets[:, :, None] == targets[:, None, :]
    earlier = jnp.arange(CLIPS)[None, :] < jnp.arange(CLIPS)[:, None]
    ranks = lax.optimization_barrier(jnp.sum(jnp.where(same & earlier[None], 1, 0), axis=2)).astype(jnp.int32)
    senders = jnp.arange(N_SRC, dtype=jnp.int32)[:, None]
    slots = (targets * (N_SRC * CAP) + senders * CAP + ranks).reshape(-1).astype(jnp.int32)
    results = lax.map(lambda clip: decode_clip(clip, conv_in, norm_gain, conv_mid, conv_up), latents)
    live = (jnp.arange(FR, dtype=jnp.int32)[None, :] < frames[:, None]).astype(jnp.float32)
    results = (results * live[:, :, None, None]).astype(jnp.bfloat16)
    output = jnp.zeros((N_SRC * N_SRC * CAP, FR, 2 * H, 2 * W * C_UP), jnp.bfloat16)
    return output.at[slots].set(results)
```

```python
import functools

import jax
import jax.numpy as jnp
from jax import lax
from jax.experimental import pallas as pl
from jax.experimental.pallas import tpu as pltpu
from jax.sharding import PartitionSpec as P

CAP = 2
FR = 4
REACH = 2
MESH = pl.DeviceIdType.MESH
BF = jnp.bfloat16
F32 = jnp.float32


def shift_down(x, first):
    return jnp.where(first, 0.0, pltpu.roll(x, 1, x.ndim - 2))


def shift_up(x, last):
    return jnp.where(last, 0.0, pltpu.roll(x, x.shape[-2] - 1, x.ndim - 2))


def exchange_kernel(
    groups, tiles, group_ref, lat_ref, cin_ref, cup_ref, recv_ref, band_ref, up_ref, out_ref, send_sem, recv_sem, fwd_send, fwd_recv
):
    src, tm, tile = lax.axis_index("src"), lax.axis_index("tm"), lax.axis_index("tile")
    clips = 4
    taps = 2 * REACH + 1

    def ok(d):
        return jnp.logical_and(tile + d >= 0, tile + d < tiles)

    partners = [(k, d) for d in (0, 1, -1, 2, -2) for k in range(groups) if (k, d) != (0, 0)]

    barrier = pltpu.get_barrier_semaphore()
    for k, d in partners:
        @pl.when(ok(d))
        def _(k=k, d=d):
            pl.semaphore_signal(
                barrier, inc=1, device_id={"src": lax.rem(src + k, groups), "tile": tile + d}, device_id_type=MESH
            )
    pl.semaphore_signal(barrier, inc=1, device_id={"tm": 1 - tm}, device_id_type=MESH)

    for g in range(groups):
        parts = []
        for k in range(CAP):
            rank_of = []
            total = jnp.zeros((lat_ref.shape[0], 128), F32)
            for i in range(clips):
                target = group_ref[src * clips + i, 0]
                rank = jnp.int32(0)
                for e in range(i):
                    rank = rank + jnp.where(group_ref[src * clips + e, 0] == target, 1, 0)
                mine = jnp.where(jnp.logical_and(target == g, rank == k), 1.0, 0.0)
                block = lat_ref[:, 128 * (i // 2) : 128 * (i // 2) + 128].astype(F32)
                if i % 2 != k:
                    block = pltpu.roll(block, 64, 1)
                total = total + block * mine
            parts.append(total)
        lane = lax.broadcasted_iota(jnp.int32, parts[0].shape, 1)
        out_ref[g] = jnp.where(lane < 64, parts[0], parts[1]).astype(BF)

    nd = jnp.int32(1)
    for d in (-2, -1, 1, 2):
        nd = nd + jnp.where(ok(d), 1, 0)
    pl.semaphore_wait(barrier, groups * nd)

    def copy(k, d):
        g = lax.rem(src + k, groups)
        return pltpu.make_async_remote_copy(
            src_ref=out_ref.at[g],
            dst_ref=recv_ref.at[tm, REACH - d, src],
            send_sem=send_sem.at[d + REACH, k],
            recv_sem=recv_sem.at[REACH - d, src],
            device_id={"src": g, "tile": tile + d},
            device_id_type=MESH,
        )

    for k, d in partners:
        @pl.when(ok(d))
        def _(k=k, d=d):
            copy(k, d).start()

    recv_ref[tm, REACH, src] = out_ref[src]

    for d in (-2, -1, 1, 2):
        @pl.when(jnp.logical_not(ok(d)))
        def _(d=d):
            recv_ref[tm, d + REACH] = jnp.zeros(recv_ref.shape[2:], BF)

    @pl.when(tm == 0)
    def _():
        recv_ref[1] = jnp.zeros(recv_ref.shape[1:], BF)

    zero = jnp.zeros((16, cin_ref.shape[-1]), BF)
    n = cin_ref.shape[-1]
    for f in range(FR):
        for c in range(3):
            for row in range(4):
                for t in range(FR):
                    for q in range(2):
                        a, b = t - f + 2, row - q
                        inside = 0 <= a <= 2 and 0 <= b <= 2
                        value = cin_ref[a, b, c] if inside else zero
                        at = ((c * 4 + row) * FR + t) * 16
                        band_ref[f, at : at + 16, q * n : (q + 1) * n] = value

    depth, width = cup_ref.shape[-2:]
    step = 96
    def fold(s, _):
        at = pl.multiple_of(s * step, step)
        for p in range(2):
            for i in range(2):
                rows = ((0,), (1, 2)) if p == 0 else ((0, 1), (2,))
                per_c = []
                for c in range(3):
                    terms = [cup_ref[b, c, pl.ds(at, step), :].astype(F32) for b in rows[i]]
                    per_c.append(functools.reduce(jnp.add, terms))
                k0, k1, k2 = per_c
                up_ref[p, pl.ds(i * depth + at, step), :] = jnp.concatenate(
                    [k1 + k2, k0 + k1, k0, k2], axis=-1
                ).astype(BF)
        return 0

    lax.fori_loop(0, depth // step, fold, 0)

    def forward(d):
        return pltpu.make_async_remote_copy(
            src_ref=recv_ref.at[0, d + REACH],
            dst_ref=recv_ref.at[0, d + REACH],
            send_sem=fwd_send.at[d + REACH],
            recv_sem=fwd_recv.at[d + REACH],
            device_id={"tm": 1 - tm},
            device_id_type=MESH,
        )

    for d in (0, 1, -1, 2, -2):
        for k in range(groups):
            if (k, d) == (0, 0):
                continue
            s = lax.rem(src + k, groups)

            @pl.when(ok(d))
            def _(d=d, s=s):
                pltpu.make_async_remote_copy(
                    src_ref=out_ref.at[0],
                    dst_ref=recv_ref.at[tm, d + REACH, s],
                    send_sem=send_sem.at[d + REACH, 0],
                    recv_sem=recv_sem.at[d + REACH, s],
                    device_id={"tm": 1 - tm},
                    device_id_type=MESH,
                ).wait_recv()

        @pl.when(tm == 0)
        def _(d=d):
            forward(d).start()

    for k, d in partners:
        @pl.when(ok(d))
        def _(k=k, d=d):
            copy(k, d).wait_send()

    for d in (0, 1, -1, 2, -2):
        @pl.when(tm == 0)
        def _(d=d):
            forward(d).wait_send()

        @pl.when(tm == 1)
        def _(d=d):
            forward(d).wait_recv()


def decode_kernel(
    groups,
    tiles,
    group_ref,
    frames_ref,
    recv_ref,
    gain_ref,
    band_hbm,
    mid_hbm,
    up_hbm,
    out_hbm,
    count_ref,
    band_ref,
    mid_ref,
    up_ref,
    z_ref,
    act_ref,
    hid_ref,
    acc_ref,
    res_ref,
    y_ref,
    o_ref,
    zero_ref,
    used_ref,
    band_sem,
    mid_sem,
    up_sem,
    zero_sem,
    o_sem,
):
    src, tm, tile = lax.axis_index("src"), lax.axis_index("tm"), lax.axis_index("tile")
    clips, slots = 4, groups * CAP
    C = gain_ref.shape[-1]
    Wd = z_ref.shape[1]
    top, bottom = tile == 0, tile == tiles - 1

    bands = [pltpu.make_async_copy(band_hbm.at[f], band_ref.at[f], band_sem.at[f]) for f in range(FR)]
    for band in bands:
        band.start()
    mids = []
    for a in (2, 1, 0):
        for b in range(3):
            for c in range(3):
                mids.append(
                    pltpu.make_async_copy(
                        mid_hbm.at[a, b, c],
                        mid_ref.at[a, pl.ds(b * C, C), pl.ds(c * C, C)],
                        mid_sem.at[a, b, c],
                    )
                )
    for mid in mids:
        mid.start()
    ups = pltpu.make_async_copy(up_hbm, up_ref, up_sem)
    ups.start()

    for s in range(slots):
        count_ref[s] = 0
    for s in range(groups):
        seen = jnp.int32(0)
        for i in range(clips):
            hit = group_ref[s * clips + i, 0] == src

            @pl.when(hit)
            def _(s=s, i=i, seen=seen):
                count_ref[s * CAP + jnp.minimum(seen, CAP - 1)] = frames_ref[s * clips + i]

            seen = seen + jnp.where(hit, 1, 0)

    zero_ref[...] = jnp.zeros(zero_ref.shape, BF)

    def clear(s, o):
        return pltpu.make_async_copy(zero_ref, out_hbm.at[s, o], zero_sem.at[s, o])

    def each_dead(go):
        def body(s, _):
            for o in range(2):
                @pl.when(2 * tm + o >= count_ref[s])
                def _():
                    go(clear(s, o))
            return 0
        lax.fori_loop(0, slots, body, 0)

    each_dead(lambda c: c.start())
    used_ref[0] = 0
    for band in bands:
        band.wait()

    lane = lax.broadcasted_iota(jnp.int32, (Wd, 128), 1)
    spot = lax.broadcasted_iota(jnp.int32, (Wd, 1), 0)
    gain = gain_ref[...]

    def first(s, _):
        n = count_ref[s]
        need = jnp.where(tm == 0, jnp.minimum(n, 2), jnp.where(n >= 3, n, 0))

        @pl.when(need > 0)
        def _():
            sender, k = s // CAP, lax.rem(s, CAP)
            for m in range(4):
                upper = [recv_ref[h, m, sender].astype(F32) for h in range(2)]
                lower = [recv_ref[h, m + 1, sender].astype(F32) for h in range(2)]
                z0 = pltpu.roll(upper[0], 96 - 64 * k, 1)
                z1 = pltpu.roll(upper[1], lax.rem(128 - 64 * k, 128), 1)
                z2 = pltpu.roll(lower[0], 64 - 64 * k, 1)
                z3 = pltpu.roll(lower[1], 96 - 64 * k, 1)
                z = jnp.where(lane < 32, z0, jnp.where(lane < 64, z1, jnp.where(lane < 96, z2, z3)))
                at = slice(128 * m, 128 * m + 128)
                z_ref[0, :, at] = shift_down(z, spot == 0).astype(BF)
                z_ref[1, :, at] = z.astype(BF)
                z_ref[2, :, at] = shift_up(z, spot == Wd - 1).astype(BF)

            for f in range(FR):
                @pl.when(f < need)
                def _(f=f):
                    lhs = jnp.concatenate(
                        [
                            jnp.concatenate([z_ref[c, :, 128 * j : 128 * j + 256] for c in range(3)], axis=1)
                            for j in range(3)
                        ],
                        axis=0,
                    )
                    h = jnp.dot(lhs, band_ref[f], preferred_element_type=F32)
                    for q in range(2):
                        hb = h[:, q * C : (q + 1) * C].astype(BF)
                        hf = hb.astype(F32)
                        ms = jnp.sum(hf * hf, axis=-1, keepdims=True) * (1.0 / C)
                        x = hf * lax.rsqrt(ms + 1e-06) * gain
                        act = x / (1.0 + jnp.exp(-x))
                        for j in range(3):
                            part = act[j * Wd : (j + 1) * Wd]
                            if j == 0:
                                part = jnp.where(top, 0.0, part)
                            if j == 2:
                                part = jnp.where(bottom, 0.0, part)
                            r = 2 * j + q
                            act_ref[s, f, r] = part.astype(BF)
                            if 1 <= r <= 4:
                                hid_ref[s, f, r - 1] = hb[j * Wd : (j + 1) * Wd]
        return 0

    lax.fori_loop(0, slots, first, 0)
    for mid in mids:
        mid.wait()
    ups.wait()

    spot4 = lax.broadcasted_iota(jnp.int32, (4, Wd, 1), 1)
    spot2 = lax.broadcasted_iota(jnp.int32, (2, Wd, 1), 1)
    left = lax.broadcasted_iota(jnp.int32, (2, Wd, C), 2) < C // 2

    def second(u, _):
        s, o = u // 2, lax.rem(u, 2)
        f = 2 * tm + o

        @pl.when(f < count_ref[s])
        def _():
            acc_ref[...] = jnp.zeros(acc_ref.shape, F32)

            def tap(a, _):
                x = act_ref[s, f - 2 + a]
                lhs = jnp.concatenate([x[b : b + 4].reshape(4 * Wd, C) for b in range(3)], axis=1)
                acc_ref[...] += jnp.dot(lhs, mid_ref[a], preferred_element_type=F32)
                return 0

            lax.fori_loop(jnp.maximum(2 - f, 0), 3, tap, 0)
            total = acc_ref[:, C : 2 * C].reshape(4, Wd, C) + hid_ref[s, f].astype(F32)
            total = total + shift_down(acc_ref[:, :C].reshape(4, Wd, C), spot4 == 0)
            total = total + shift_up(acc_ref[:, 2 * C :].reshape(4, Wd, C), spot4 == Wd - 1)
            for r in range(4):
                part = total[r]
                if r == 0:
                    part = jnp.where(top, 0.0, part)
                if r == 3:
                    part = jnp.where(bottom, 0.0, part)
                res_ref[r] = part.astype(BF)

            for p in range(2):
                lhs = jnp.concatenate(
                    [res_ref[p : p + 2].reshape(2 * Wd, C), res_ref[p + 1 : p + 3].reshape(2 * Wd, C)], axis=1
                )
                y = jnp.dot(lhs, up_ref[p], preferred_element_type=F32)
                still = y[:, :C].reshape(2, Wd, C)
                moved = y[:, C:].reshape(2, Wd, C)
                y = still + jnp.where(left, shift_down(moved, spot2 == 0), shift_up(moved, spot2 == Wd - 1))
                for h in range(2):
                    for v in range(C // 128):
                        y_ref[v, pl.ds((2 * h + p) * Wd, Wd), :] = y[h, :, v * 128 : v * 128 + 128]

            used = used_ref[0]
            buf = lax.rem(used, 2)

            @pl.when(used >= 2)
            def _():
                pltpu.make_async_copy(o_ref.at[buf], out_hbm.at[s, o], o_sem.at[buf]).wait()

            for w in range(Wd):
                for v in range(C // 128):
                    at = w * C + v * 128
                    o_ref[buf, :, at : at + 128] = y_ref[v, pl.ds(w, 4, stride=Wd), :].astype(BF)
            pltpu.make_async_copy(o_ref.at[buf], out_hbm.at[s, o], o_sem.at[buf]).start()
            used_ref[0] = used + 1
        return 0

    lax.fori_loop(0, 2 * slots, second, 0)

    used = used_ref[0]
    for last in range(2):
        @pl.when(used > last)
        def _(last=last):
            buf = lax.rem(used - 1 - last, 2)
            pltpu.make_async_copy(o_ref.at[buf], out_hbm.at[0, 0], o_sem.at[buf]).wait()
    each_dead(lambda c: c.wait())


def per_device(latents, decoder_group, frames, conv_in, norm_gain, conv_mid, conv_up):
    groups, tiles = lax.axis_size("src"), lax.axis_size("tile")
    clips, slab, rows, packed = latents.shape
    lc, C = conv_in.shape[3:]
    width = packed // lc
    out_c = conv_up.shape[-1]
    slots = groups * CAP
    lat = latents.reshape(clips, slab, rows, width, lc).transpose(3, 0, 2, 1, 4).reshape(width, -1)
    vmem = pl.BlockSpec(memory_space=pltpu.VMEM)
    smem = pl.BlockSpec(memory_space=pltpu.SMEM)
    hbm = pl.BlockSpec(memory_space=pl.ANY)
    taps = 2 * REACH + 1
    recv, band, up = pl.pallas_call(
        functools.partial(exchange_kernel, groups, tiles),
        out_shape=(
            jax.ShapeDtypeStruct((2, taps, groups, width, 128), BF),
            jax.ShapeDtypeStruct((FR, 3 * 4 * FR * lc, 2 * C), BF),
            jax.ShapeDtypeStruct((2, 2 * C, 4 * out_c), BF),
        ),
        in_specs=[smem, vmem, vmem, vmem],
        out_specs=(vmem, vmem, vmem),
        scratch_shapes=[
            pltpu.VMEM((groups, width, 128), BF),
            pltpu.SemaphoreType.DMA((taps, groups)),
            pltpu.SemaphoreType.DMA((taps, groups)),
            pltpu.SemaphoreType.DMA((taps,)),
            pltpu.SemaphoreType.DMA((taps,)),
        ],
        compiler_params=pltpu.CompilerParams(
            collective_id=0, has_side_effects=True, vmem_limit_bytes=32 * 1024 * 1024
        ),
    )(decoder_group, lat, conv_in, conv_up)

    return pl.pallas_call(
        functools.partial(decode_kernel, groups, tiles),
        out_shape=jax.ShapeDtypeStruct((slots, slab, 2 * rows, 2 * width * out_c), BF),
        in_specs=[smem, smem, vmem, vmem, hbm, hbm, hbm],
        out_specs=hbm,
        scratch_shapes=[
            pltpu.SMEM((slots,), jnp.int32),
            pltpu.VMEM(band.shape, BF),
            pltpu.VMEM((3, 3 * C, 3 * C), BF),
            pltpu.VMEM(up.shape, BF),
            pltpu.VMEM((3, width, 4 * FR * lc * 2), BF),
            pltpu.VMEM((slots, FR, 6, width, C), BF),
            pltpu.VMEM((slots, FR, 4, width, C), BF),
            pltpu.VMEM((4 * width, 3 * C), F32),
            pltpu.VMEM((4, width, C), BF),
            pltpu.VMEM((C // 128, 4 * width, 128), F32),
            pltpu.VMEM((2, 2 * rows, 2 * width * out_c), BF),
            pltpu.VMEM((2 * rows, 2 * width * out_c), BF),
            pltpu.SMEM((1,), jnp.int32),
            pltpu.SemaphoreType.DMA((FR,)),
            pltpu.SemaphoreType.DMA((3, 3, 3)),
            pltpu.SemaphoreType.DMA,
            pltpu.SemaphoreType.DMA((slots, 2)),
            pltpu.SemaphoreType.DMA((2,)),
        ],
        compiler_params=pltpu.CompilerParams(vmem_limit_bytes=56 * 1024 * 1024),
    )(decoder_group, frames, recv, norm_gain.reshape(1, C), band, conv_mid, up)


def solution(mesh):
    placed = (P("src", "tm", "tile", None), P(), P(), P(), P(), P(), P())
    return jax.shard_map(
        per_device,
        mesh=mesh,
        in_specs=placed,
        out_specs=P("src", "tm", "tile", None),
        check_vma=False,
    )
```

```python
import functools

import jax
import jax.numpy as jnp
from jax import lax
from jax.experimental import pallas as pl
from jax.experimental.pallas import tpu as pltpu
from jax.sharding import PartitionSpec as P

CAP = 2
FR = 4
REACH = 2
MESH = pl.DeviceIdType.MESH
BF = jnp.bfloat16
F32 = jnp.float32


def shift_down(x, first):
    return jnp.where(first, 0.0, pltpu.roll(x, 1, x.ndim - 2))


def shift_up(x, last):
    return jnp.where(last, 0.0, pltpu.roll(x, x.shape[-2] - 1, x.ndim - 2))


def exchange_kernel(
    groups,
    tiles,
    group_ref,
    lat_ref,
    cin_ref,
    cup_ref,
    mid_hbm,
    recv_ref,
    band_ref,
    up_ref,
    mid_ref,
    out_ref,
    send_sem,
    recv_sem,
    fwd_send,
    fwd_recv,
    mid_sem,
):
    src, tm, tile = lax.axis_index("src"), lax.axis_index("tm"), lax.axis_index("tile")
    clips = 4
    taps = 2 * REACH + 1

    def ok(d):
        return jnp.logical_and(tile + d >= 0, tile + d < tiles)

    partners = [(k, d) for d in (0, 1, -1, 2, -2) for k in range(groups) if (k, d) != (0, 0)]

    n = cin_ref.shape[-1]
    mids = [
        pltpu.make_async_copy(
            mid_hbm.at[a, b, c], mid_ref.at[a, pl.ds(b * n, n), pl.ds(c * n, n)], mid_sem.at[a, b, c]
        )
        for a in (2, 1, 0)
        for b in range(3)
        for c in range(3)
    ]
    for mid in mids:
        mid.start()

    barrier = pltpu.get_barrier_semaphore()
    for k, d in partners:
        @pl.when(ok(d))
        def _(k=k, d=d):
            pl.semaphore_signal(
                barrier, inc=1, device_id={"src": lax.rem(src + k, groups), "tile": tile + d}, device_id_type=MESH
            )
    pl.semaphore_signal(barrier, inc=1, device_id={"tm": 1 - tm}, device_id_type=MESH)

    for g in range(groups):
        parts = []
        for k in range(CAP):
            rank_of = []
            total = jnp.zeros((lat_ref.shape[0], 128), F32)
            for i in range(clips):
                target = group_ref[src * clips + i]
                rank = jnp.int32(0)
                for e in range(i):
                    rank = rank + jnp.where(group_ref[src * clips + e] == target, 1, 0)
                mine = jnp.where(jnp.logical_and(target == g, rank == k), 1.0, 0.0)
                block = lat_ref[:, 128 * (i // 2) : 128 * (i // 2) + 128].astype(F32)
                if i % 2 != k:
                    block = pltpu.roll(block, 64, 1)
                total = total + block * mine
            parts.append(total)
        lane = lax.broadcasted_iota(jnp.int32, parts[0].shape, 1)
        out_ref[g] = jnp.where(lane < 64, parts[0], parts[1]).astype(BF)

    nd = jnp.int32(1)
    for d in (-2, -1, 1, 2):
        nd = nd + jnp.where(ok(d), 1, 0)
    pl.semaphore_wait(barrier, groups * nd)

    def copy(k, d):
        g = lax.rem(src + k, groups)
        return pltpu.make_async_remote_copy(
            src_ref=out_ref.at[g],
            dst_ref=recv_ref.at[tm, REACH - d, src],
            send_sem=send_sem.at[d + REACH, k],
            recv_sem=recv_sem.at[REACH - d, src],
            device_id={"src": g, "tile": tile + d},
            device_id_type=MESH,
        )

    for k, d in partners:
        @pl.when(ok(d))
        def _(k=k, d=d):
            copy(k, d).start()

    recv_ref[tm, REACH, src] = out_ref[src]

    for d in (-2, -1, 1, 2):
        @pl.when(jnp.logical_not(ok(d)))
        def _(d=d):
            recv_ref[tm, d + REACH] = jnp.zeros(recv_ref.shape[2:], BF)

    @pl.when(tm == 0)
    def _():
        recv_ref[1] = jnp.zeros(recv_ref.shape[1:], BF)

    zero = jnp.zeros((16, cin_ref.shape[-1]), BF)
    for f in range(FR):
        for c in range(3):
            for row in range(4):
                for t in range(FR):
                    for q in range(2):
                        a, b = t - f + 2, row - q
                        inside = 0 <= a <= 2 and 0 <= b <= 2
                        value = cin_ref[a, b, c] if inside else zero
                        at = ((c * 4 + row) * FR + t) * 16
                        band_ref[f, at : at + 16, q * n : (q + 1) * n] = value

    def fold():
        width, depth = cup_ref.shape[-2:]
        for p in range(2):
            for i in range(2):
                rows = ((0,), (1, 2)) if p == 0 else ((0, 1), (2,))
                k0, k1, k2 = [
                    functools.reduce(jnp.add, [cup_ref[b, c].astype(F32) for b in rows[i]]) for c in range(3)
                ]
                for at, value in enumerate((k1 + k2, k0 + k1, k0, k2)):
                    up_ref[p, at * width : (at + 1) * width, i * depth : (i + 1) * depth] = value.astype(BF)

    def forward(d):
        return pltpu.make_async_remote_copy(
            src_ref=recv_ref.at[0, d + REACH],
            dst_ref=recv_ref.at[0, d + REACH],
            send_sem=fwd_send.at[d + REACH],
            recv_sem=fwd_recv.at[d + REACH],
            device_id={"tm": 1 - tm},
            device_id_type=MESH,
        )

    for d in (0, 1, -1, 2, -2):
        for k in range(groups):
            if (k, d) == (0, 0):
                continue
            s = lax.rem(src + k, groups)

            @pl.when(ok(d))
            def _(d=d, s=s):
                pltpu.make_async_remote_copy(
                    src_ref=out_ref.at[0],
                    dst_ref=recv_ref.at[tm, d + REACH, s],
                    send_sem=send_sem.at[d + REACH, 0],
                    recv_sem=recv_sem.at[d + REACH, s],
                    device_id={"tm": 1 - tm},
                    device_id_type=MESH,
                ).wait_recv()

        @pl.when(tm == 0)
        def _(d=d):
            forward(d).start()

    fold()

    for k, d in partners:
        @pl.when(ok(d))
        def _(k=k, d=d):
            copy(k, d).wait_send()

    for d in (0, 1, -1, 2, -2):
        @pl.when(tm == 0)
        def _(d=d):
            forward(d).wait_send()

        @pl.when(tm == 1)
        def _(d=d):
            forward(d).wait_recv()

    for mid in mids:
        mid.wait()


def decode_kernel(
    groups,
    tiles,
    group_ref,
    frames_ref,
    recv_ref,
    gain_ref,
    band_ref,
    mid_ref,
    up_ref,
    out_hbm,
    count_ref,
    z_ref,
    act_ref,
    hid_ref,
    acc_ref,
    res_ref,
    y_ref,
    o_ref,
    zero_ref,
    used_ref,
    zero_sem,
    o_sem,
):
    src, tm, tile = lax.axis_index("src"), lax.axis_index("tm"), lax.axis_index("tile")
    clips, slots = 4, groups * CAP
    C = gain_ref.shape[-1]
    Wd = z_ref.shape[1]
    top, bottom = tile == 0, tile == tiles - 1

    for s in range(slots):
        count_ref[s] = 0
    for s in range(groups):
        seen = jnp.int32(0)
        for i in range(clips):
            hit = group_ref[s * clips + i] == src

            @pl.when(hit)
            def _(s=s, i=i, seen=seen):
                count_ref[s * CAP + jnp.minimum(seen, CAP - 1)] = frames_ref[s * clips + i]

            seen = seen + jnp.where(hit, 1, 0)

    zero_ref[...] = jnp.zeros(zero_ref.shape, BF)

    def clear(s, o):
        return pltpu.make_async_copy(zero_ref, out_hbm.at[s, o], zero_sem.at[s, o])

    def each_dead(go):
        def body(s, _):
            for o in range(2):
                @pl.when(2 * tm + o >= count_ref[s])
                def _():
                    go(clear(s, o))
            return 0
        lax.fori_loop(0, slots, body, 0)

    each_dead(lambda c: c.start())
    used_ref[0] = 0

    lane = lax.broadcasted_iota(jnp.int32, (Wd, 128), 1)
    spot = lax.broadcasted_iota(jnp.int32, (Wd, 1), 0)
    gain = gain_ref[...].reshape(1, C)

    def first(s, _):
        n = count_ref[s]
        need = jnp.where(tm == 0, jnp.minimum(n, 2), jnp.where(n >= 3, n, 0))

        @pl.when(need > 0)
        def _():
            sender, k = s // CAP, lax.rem(s, CAP)
            for m in range(4):
                upper = [recv_ref[h, m, sender].astype(F32) for h in range(2)]
                lower = [recv_ref[h, m + 1, sender].astype(F32) for h in range(2)]
                z0 = pltpu.roll(upper[0], 96 - 64 * k, 1)
                z1 = pltpu.roll(upper[1], lax.rem(128 - 64 * k, 128), 1)
                z2 = pltpu.roll(lower[0], 64 - 64 * k, 1)
                z3 = pltpu.roll(lower[1], 96 - 64 * k, 1)
                z = jnp.where(lane < 32, z0, jnp.where(lane < 64, z1, jnp.where(lane < 96, z2, z3)))
                at = slice(128 * m, 128 * m + 128)
                z_ref[0, :, at] = shift_down(z, spot == 0).astype(BF)
                z_ref[1, :, at] = z.astype(BF)
                z_ref[2, :, at] = shift_up(z, spot == Wd - 1).astype(BF)

            for f in range(FR):
                @pl.when(f < need)
                def _(f=f):
                    lhs = jnp.concatenate(
                        [
                            jnp.concatenate([z_ref[c, :, 128 * j : 128 * j + 256] for c in range(3)], axis=1)
                            for j in range(3)
                        ],
                        axis=0,
                    )
                    h = jnp.dot(lhs, band_ref[f], preferred_element_type=F32)
                    for q in range(2):
                        hb = h[:, q * C : (q + 1) * C].astype(BF)
                        hf = hb.astype(F32)
                        ms = jnp.sum(hf * hf, axis=-1, keepdims=True) * (1.0 / C)
                        x = hf * (0.5 * lax.rsqrt(ms + 1e-06)) * gain
                        act = x + x * jnp.tanh(x)
                        for j in range(3):
                            part = act[j * Wd : (j + 1) * Wd]
                            if j == 0:
                                part = jnp.where(top, 0.0, part)
                            if j == 2:
                                part = jnp.where(bottom, 0.0, part)
                            r = 2 * j + q
                            act_ref[s, f, r] = part.astype(BF)
                            if 1 <= r <= 4:
                                hid_ref[s, f, r - 1] = hb[j * Wd : (j + 1) * Wd]
        return 0

    lax.fori_loop(0, slots, first, 0)
    spot4 = lax.broadcasted_iota(jnp.int32, (4, Wd, 1), 1)
    spot2 = lax.broadcasted_iota(jnp.int32, (2, Wd, 1), 1)
    left = lax.broadcasted_iota(jnp.int32, (2, Wd, C), 2) < C // 2

    def second(u, _):
        s, o = u // 2, lax.rem(u, 2)
        f = 2 * tm + o

        @pl.when(f < count_ref[s])
        def _():
            for taps in range(1, 4):
                @pl.when(taps == jnp.minimum(f + 1, 3))
                def _():
                    lhs = jnp.concatenate(
                        [act_ref[s, f + a - 2, b : b + 4].reshape(4 * Wd, C) for a in range(3 - taps, 3) for b in range(3)],
                        axis=1,
                    )
                    rhs = mid_ref[3 - taps :].reshape(taps * 3 * C, 3 * C)
                    acc_ref[...] = jnp.dot(lhs, rhs, preferred_element_type=F32)

            total = acc_ref[:, C : 2 * C].reshape(4, Wd, C) + hid_ref[s, f].astype(F32)
            total = total + shift_down(acc_ref[:, :C].reshape(4, Wd, C), spot4 == 0)
            total = total + shift_up(acc_ref[:, 2 * C :].reshape(4, Wd, C), spot4 == Wd - 1)
            for r in range(4):
                part = total[r]
                if r == 0:
                    part = jnp.where(top, 0.0, part)
                if r == 3:
                    part = jnp.where(bottom, 0.0, part)
                res_ref[r] = part.astype(BF)

            for p in range(2):
                lhs = jnp.concatenate(
                    [res_ref[p : p + 2].reshape(2 * Wd, C), res_ref[p + 1 : p + 3].reshape(2 * Wd, C)], axis=1
                )
                y = lax.dot_general(lhs, up_ref[p], (((1,), (1,)), ((), ())), preferred_element_type=F32)
                still = y[:, :C].reshape(2, Wd, C)
                moved = y[:, C:].reshape(2, Wd, C)
                y = still + jnp.where(left, shift_down(moved, spot2 == 0), shift_up(moved, spot2 == Wd - 1))
                for h in range(2):
                    for v in range(C // 128):
                        y_ref[v, pl.ds((2 * h + p) * Wd, Wd), :] = y[h, :, v * 128 : v * 128 + 128]

            used = used_ref[0]
            buf = lax.rem(used, 2)

            @pl.when(used >= 2)
            def _():
                pltpu.make_async_copy(o_ref.at[buf], out_hbm.at[s, o], o_sem.at[buf]).wait()

            for w in range(Wd):
                for v in range(C // 128):
                    at = w * C + v * 128
                    o_ref[buf, :, at : at + 128] = y_ref[v, pl.ds(w, 4, stride=Wd), :].astype(BF)
            pltpu.make_async_copy(o_ref.at[buf], out_hbm.at[s, o], o_sem.at[buf]).start()
            used_ref[0] = used + 1
        return 0

    lax.fori_loop(0, 2 * slots, second, 0)

    used = used_ref[0]
    for last in range(2):
        @pl.when(used > last)
        def _(last=last):
            buf = lax.rem(used - 1 - last, 2)
            pltpu.make_async_copy(o_ref.at[buf], out_hbm.at[0, 0], o_sem.at[buf]).wait()
    each_dead(lambda c: c.wait())


def per_device(latents, decoder_group, frames, conv_in, norm_gain, conv_mid, conv_up):
    groups, tiles = lax.axis_size("src"), lax.axis_size("tile")
    clips, slab, rows, packed = latents.shape
    lc, C = conv_in.shape[3:]
    width = packed // lc
    out_c = conv_up.shape[-1]
    slots = groups * CAP
    lat = latents.reshape(clips, slab, rows, width, lc).transpose(3, 0, 2, 1, 4).reshape(width, -1)
    group = decoder_group.reshape(-1)
    vmem = pl.BlockSpec(memory_space=pltpu.VMEM)
    smem = pl.BlockSpec(memory_space=pltpu.SMEM)
    hbm = pl.BlockSpec(memory_space=pltpu.HBM)
    taps = 2 * REACH + 1
    recv, band, up, mid = pl.pallas_call(
        functools.partial(exchange_kernel, groups, tiles),
        out_shape=(
            jax.ShapeDtypeStruct((2, taps, groups, width, 128), BF),
            jax.ShapeDtypeStruct((FR, 3 * 4 * FR * lc, 2 * C), BF),
            jax.ShapeDtypeStruct((2, 4 * out_c, 2 * C), BF),
            jax.ShapeDtypeStruct((3, 3 * C, 3 * C), BF),
        ),
        in_specs=[smem, vmem, vmem, vmem, hbm],
        out_specs=(vmem, vmem, vmem, vmem),
        scratch_shapes=[
            pltpu.VMEM((groups, width, 128), BF),
            pltpu.SemaphoreType.DMA((taps, groups)),
            pltpu.SemaphoreType.DMA((taps, groups)),
            pltpu.SemaphoreType.DMA((taps,)),
            pltpu.SemaphoreType.DMA((taps,)),
            pltpu.SemaphoreType.DMA((3, 3, 3)),
        ],
        compiler_params=pltpu.CompilerParams(
            collective_id=0, has_side_effects=True, vmem_limit_bytes=33 * 1024 * 1024
        ),
    )(group, lat, conv_in, conv_up.transpose(0, 1, 3, 2), conv_mid)

    return pl.pallas_call(
        functools.partial(decode_kernel, groups, tiles),
        out_shape=jax.ShapeDtypeStruct((slots, slab, 2 * rows, 2 * width * out_c), BF),
        in_specs=[smem, smem, vmem, vmem, vmem, vmem, vmem],
        out_specs=hbm,
        scratch_shapes=[
            pltpu.SMEM((slots,), jnp.int32),
            pltpu.VMEM((3, width, 4 * FR * lc * 2), BF),
            pltpu.VMEM((slots, FR, 6, width, C), BF),
            pltpu.VMEM((slots, FR, 4, width, C), BF),
            pltpu.VMEM((4 * width, 3 * C), F32),
            pltpu.VMEM((4, width, C), BF),
            pltpu.VMEM((C // 128, 4 * width, 128), F32),
            pltpu.VMEM((2, 2 * rows, 2 * width * out_c), BF),
            pltpu.VMEM((2 * rows, 2 * width * out_c), BF),
            pltpu.SMEM((1,), jnp.int32),
            pltpu.SemaphoreType.DMA((slots, 2)),
            pltpu.SemaphoreType.DMA((2,)),
        ],
        compiler_params=pltpu.CompilerParams(vmem_limit_bytes=24 * 1024 * 1024),
    )(group, frames, recv, norm_gain, band, mid, up)


def solution(mesh):
    placed = (P("src", "tm", "tile", None), P(), P(), P(), P(), P(), P())
    return jax.shard_map(
        per_device,
        mesh=mesh,
        in_specs=placed,
        out_specs=P("src", "tm", "tile", None),
        check_vma=False,
    )
```

```python
import functools

import jax
import jax.numpy as jnp
from jax import lax
from jax.experimental import pallas as pl
from jax.experimental.pallas import tpu as pltpu
from jax.sharding import PartitionSpec as P

CAP = 2
FR = 4
REACH = 2
MESH = pl.DeviceIdType.MESH
BF = jnp.bfloat16
F32 = jnp.float32


def shift_down(x, first):
    return jnp.where(first, 0.0, pltpu.roll(x, 1, x.ndim - 2))


def shift_up(x, last):
    return jnp.where(last, 0.0, pltpu.roll(x, x.shape[-2] - 1, x.ndim - 2))


def exchange_kernel(
    groups, tiles, group_ref, lat_ref, recv_ref, out_ref, send_sem, recv_sem, fwd_send, fwd_recv
):
    src, tm, tile = lax.axis_index("src"), lax.axis_index("tm"), lax.axis_index("tile")
    clips = 4

    def ok(d):
        return jnp.logical_and(tile + d >= 0, tile + d < tiles)

    partners = [(k, d) for d in (2, -2, 1, -1, 0) for k in (2, 1, 3, 0) if (k, d) != (0, 0)]

    barrier = pltpu.get_barrier_semaphore()
    for k, d in partners:
        @pl.when(ok(d))
        def _(k=k, d=d):
            pl.semaphore_signal(
                barrier, inc=1, device_id={"src": lax.rem(src + k, groups), "tile": tile + d}, device_id_type=MESH
            )
    pl.semaphore_signal(barrier, inc=1, device_id={"tm": 1 - tm}, device_id_type=MESH)

    blocks = []
    for i in range(clips):
        block = lat_ref[:, 128 * (i // 2) : 128 * (i // 2) + 128].astype(F32)
        blocks.append((block, pltpu.roll(block, 64, 1)))
    lane = lax.broadcasted_iota(jnp.int32, blocks[0][0].shape, 1)
    targets = [group_ref[src * clips + i] for i in range(clips)]
    ranks = []
    for i in range(clips):
        rank = jnp.int32(0)
        for e in range(i):
            rank = rank + jnp.where(targets[e] == targets[i], 1, 0)
        ranks.append(rank)
    for g in range(groups):
        parts = []
        for k in range(CAP):
            total = jnp.zeros(lane.shape, F32)
            for i in range(clips):
                mine = jnp.logical_and(targets[i] == g, ranks[i] == k)
                total = total + blocks[i][(i + k) % 2] * jnp.where(mine, 1.0, 0.0)
            parts.append(total)
        out_ref[g] = jnp.where(lane < 64, parts[0], parts[1]).astype(BF)

    for d in (-2, -1, 1, 2):
        @pl.when(jnp.logical_not(ok(d)))
        def _(d=d):
            recv_ref[tm, d + REACH] = jnp.zeros(recv_ref.shape[2:], BF)

    @pl.when(tm == 0)
    def _():
        recv_ref[1] = jnp.zeros(recv_ref.shape[1:], BF)

    recv_ref[tm, REACH, src] = out_ref[src]

    nd = jnp.int32(1)
    for d in (-2, -1, 1, 2):
        nd = nd + jnp.where(ok(d), 1, 0)
    pl.semaphore_wait(barrier, groups * nd)

    def copy(k, d):
        g = lax.rem(src + k, groups)
        return pltpu.make_async_remote_copy(
            src_ref=out_ref.at[g],
            dst_ref=recv_ref.at[tm, REACH - d, src],
            send_sem=send_sem.at[d + REACH, k],
            recv_sem=recv_sem.at[REACH - d, src],
            device_id={"src": g, "tile": tile + d},
            device_id_type=MESH,
        )

    for k, d in partners:
        @pl.when(ok(d))
        def _(k=k, d=d):
            copy(k, d).start()

    def forward(d):
        return pltpu.make_async_remote_copy(
            src_ref=recv_ref.at[0, d + REACH],
            dst_ref=recv_ref.at[0, d + REACH],
            send_sem=fwd_send.at[d + REACH],
            recv_sem=fwd_recv.at[d + REACH],
            device_id={"tm": 1 - tm},
            device_id_type=MESH,
        )

    for d in (0, 1, -1, 2, -2):
        for k in range(groups):
            if (k, d) == (0, 0):
                continue
            s = lax.rem(src + k, groups)

            @pl.when(ok(d))
            def _(d=d, s=s):
                pltpu.make_async_remote_copy(
                    src_ref=out_ref.at[0],
                    dst_ref=recv_ref.at[tm, d + REACH, s],
                    send_sem=send_sem.at[d + REACH, 0],
                    recv_sem=recv_sem.at[d + REACH, s],
                    device_id={"tm": 1 - tm},
                    device_id_type=MESH,
                ).wait_recv()

        @pl.when(tm == 0)
        def _(d=d):
            forward(d).start()

    for k, d in partners:
        @pl.when(ok(d))
        def _(k=k, d=d):
            copy(k, d).wait_send()

    for d in (0, 1, -1, 2, -2):
        @pl.when(tm == 0)
        def _(d=d):
            forward(d).wait_send()

        @pl.when(tm == 1)
        def _(d=d):
            forward(d).wait_recv()


def decode_kernel(
    groups,
    tiles,
    group_ref,
    frames_ref,
    recv_ref,
    gain_ref,
    cin_ref,
    mid_ref,
    cup_ref,
    out_hbm,
    count_ref,
    up_ref,
    turn_ref,
    z_ref,
    act_ref,
    hid_ref,
    acc_ref,
    res_ref,
    y_ref,
    o_ref,
    zero_ref,
    used_ref,
    zero_sem,
    o_sem,
):
    src, tm, tile = lax.axis_index("src"), lax.axis_index("tm"), lax.axis_index("tile")
    clips, slots = 4, groups * CAP
    C = gain_ref.shape[-1]
    Wd = z_ref.shape[1]
    top, bottom = tile == 0, tile == tiles - 1

    for s in range(slots):
        count_ref[s] = 0
    for s in range(groups):
        seen = jnp.int32(0)
        for i in range(clips):
            hit = group_ref[s * clips + i] == src

            @pl.when(hit)
            def _(s=s, i=i, seen=seen):
                count_ref[s * CAP + jnp.minimum(seen, CAP - 1)] = frames_ref[s * clips + i]

            seen = seen + jnp.where(hit, 1, 0)

    zero_ref[...] = jnp.zeros(zero_ref.shape, BF)

    def clear(s, o):
        return pltpu.make_async_copy(zero_ref, out_hbm.at[s, o], zero_sem.at[s, o])

    def each_dead(go):
        def body(s, _):
            for o in range(2):
                @pl.when(2 * tm + o >= count_ref[s])
                def _():
                    go(clear(s, o))
            return 0
        lax.fori_loop(0, slots, body, 0)

    each_dead(lambda c: c.start())

    width = cup_ref.shape[-2]
    for p in range(2):
        for i in range(2):
            rows = ((0,), (1, 2)) if p == 0 else ((0, 1), (2,))
            k0, k1, k2 = [
                functools.reduce(jnp.add, [cup_ref[b, c].astype(F32) for b in rows[i]]) for c in range(3)
            ]
            for at, value in enumerate((k1 + k2, k0 + k1, k0, k2)):
                turn_ref[at * width : (at + 1) * width, :] = value.astype(BF)
            up_ref[p, i * C : (i + 1) * C, :] = turn_ref[...].T

    lane = lax.broadcasted_iota(jnp.int32, (Wd, 128), 1)
    spot = lax.broadcasted_iota(jnp.int32, (Wd, 1), 0)
    gain = gain_ref[...].reshape(1, C)
    nothing = jnp.zeros((16, C), BF)

    def band(f):
        rows = []
        for c in range(3):
            for row in range(4):
                for t in range(FR):
                    a = t - f + 2
                    rows.append(
                        jnp.concatenate(
                            [
                                cin_ref[a, row - q, c] if 0 <= a <= 2 and 0 <= row - q <= 2 else nothing
                                for q in range(2)
                            ],
                            axis=1,
                        )
                    )
        return jnp.concatenate(rows, axis=0)

    def hidden(s, frames):
        lhs = jnp.concatenate(
            [
                jnp.concatenate([z_ref[c, :, 128 * j : 128 * j + 256] for c in range(3)], axis=1)
                for j in range(3)
            ],
            axis=0,
        )
        for f in frames:
            h = jnp.dot(lhs, band(f), preferred_element_type=F32)
            for q in range(2):
                hb = h[:, q * C : (q + 1) * C].astype(BF)
                hf = hb.astype(F32)
                ms = jnp.sum(hf * hf, axis=-1, keepdims=True) * (1.0 / C)
                x = hf * (0.5 * lax.rsqrt(ms + 1e-06)) * gain
                act = x + x * jnp.tanh(x)
                for j in range(3):
                    part = act[j * Wd : (j + 1) * Wd]
                    if j == 0:
                        part = jnp.where(top, 0.0, part)
                    if j == 2:
                        part = jnp.where(bottom, 0.0, part)
                    r = 2 * j + q
                    act_ref[s, f, r] = part.astype(BF)
                    if 1 <= r <= 4:
                        hid_ref[s, f, r - 1] = hb[j * Wd : (j + 1) * Wd]

    def first(s, _):
        n = count_ref[s]
        need = jnp.where(tm == 0, jnp.minimum(n, 2), jnp.where(n >= 3, n, 0))

        @pl.when(need > 0)
        def _():
            sender, k = s // CAP, lax.rem(s, CAP)
            for m in range(4):
                upper = [recv_ref[h, m, sender].astype(F32) for h in range(2)]
                lower = [recv_ref[h, m + 1, sender].astype(F32) for h in range(2)]
                z0 = pltpu.roll(upper[0], 96 - 64 * k, 1)
                z1 = pltpu.roll(upper[1], lax.rem(128 - 64 * k, 128), 1)
                z2 = pltpu.roll(lower[0], 64 - 64 * k, 1)
                z3 = pltpu.roll(lower[1], 96 - 64 * k, 1)
                z = jnp.where(lane < 32, z0, jnp.where(lane < 64, z1, jnp.where(lane < 96, z2, z3)))
                at = slice(128 * m, 128 * m + 128)
                z_ref[0, :, at] = shift_down(z, spot == 0).astype(BF)
                z_ref[1, :, at] = z.astype(BF)
                z_ref[2, :, at] = shift_up(z, spot == Wd - 1).astype(BF)

        for frames, when in (
            ((0,), need == 1),
            ((0, 1), need >= 2),
            ((2,), need == 3),
            ((2, 3), need == 4),
        ):
            @pl.when(when)
            def _(frames=frames):
                hidden(s, frames)
        return 0

    lax.fori_loop(0, slots, first, 0)

    spot4 = lax.broadcasted_iota(jnp.int32, (4, Wd, 1), 1)
    spot2 = lax.broadcasted_iota(jnp.int32, (2, Wd, 1), 1)
    left = lax.broadcasted_iota(jnp.int32, (2, Wd, C), 2) < C // 2
    for e in range(5):
        used_ref[e] = 0

    def drain(buf):
        for e in range(2):
            @pl.when(used_ref[1 + 2 * buf + e] == 1)
            def _(e=e):
                pltpu.make_async_copy(o_ref.at[buf, e], out_hbm.at[0, 0], o_sem.at[buf, e]).wait()
                used_ref[1 + 2 * buf + e] = 0

    def finish(s, units):
        count = len(units)
        used = used_ref[0]
        buf = lax.rem(used, 2)
        for e, (o, taps) in enumerate(units):
            f = 2 * tm + o
            lhs = jnp.concatenate(
                [act_ref[s, f + a - 2, b : b + 4].reshape(4 * Wd, C) for a in range(3 - taps, 3) for b in range(3)],
                axis=1,
            )
            rhs = jnp.concatenate(
                [
                    jnp.concatenate([mid_ref[a, b, c] for c in range(3)], axis=1)
                    for a in range(3 - taps, 3)
                    for b in range(3)
                ],
                axis=0,
            )
            acc_ref[e] = jnp.dot(lhs, rhs, preferred_element_type=F32)

        drain(buf)

        for e, (o, taps) in enumerate(units):
            f = 2 * tm + o
            total = acc_ref[e, :, C : 2 * C].reshape(4, Wd, C) + hid_ref[s, f].astype(F32)
            total = total + shift_down(acc_ref[e, :, :C].reshape(4, Wd, C), spot4 == 0)
            total = total + shift_up(acc_ref[e, :, 2 * C :].reshape(4, Wd, C), spot4 == Wd - 1)
            for r in range(4):
                part = total[r]
                if r == 0:
                    part = jnp.where(top, 0.0, part)
                if r == 3:
                    part = jnp.where(bottom, 0.0, part)
                res_ref[e, r] = part.astype(BF)

        for p in range(2):
            lhs = jnp.concatenate(
                [
                    jnp.concatenate(
                        [res_ref[e, p : p + 2].reshape(2 * Wd, C), res_ref[e, p + 1 : p + 3].reshape(2 * Wd, C)],
                        axis=1,
                    )
                    for e in range(count)
                ],
                axis=0,
            )
            both = jnp.dot(lhs, up_ref[p], preferred_element_type=F32)
            for e in range(count):
                y = both[e * 2 * Wd : (e + 1) * 2 * Wd]
                still = y[:, :C].reshape(2, Wd, C)
                moved = y[:, C:].reshape(2, Wd, C)
                y = still + jnp.where(left, shift_down(moved, spot2 == 0), shift_up(moved, spot2 == Wd - 1))
                for h in range(2):
                    for v in range(C // 128):
                        y_ref[e, v, pl.ds((2 * h + p) * Wd, Wd), :] = y[h, :, v * 128 : v * 128 + 128]

        for e, (o, taps) in enumerate(units):
            for w in range(Wd):
                for v in range(C // 128):
                    at = w * C + v * 128
                    o_ref[buf, e, :, at : at + 128] = y_ref[e, v, pl.ds(w, 4, stride=Wd), :].astype(BF)
            pltpu.make_async_copy(o_ref.at[buf, e], out_hbm.at[s, o], o_sem.at[buf, e]).start()
            used_ref[1 + 2 * buf + e] = 1
        used_ref[0] = used + 1

    def second(s, _):
        n = count_ref[s]
        for units, when in (
            (((0, 1),), jnp.logical_and(tm == 0, n == 1)),
            (((0, 1), (1, 2)), jnp.logical_and(tm == 0, n >= 2)),
            (((0, 3),), jnp.logical_and(tm == 1, n == 3)),
            (((0, 3), (1, 3)), jnp.logical_and(tm == 1, n >= 4)),
        ):
            @pl.when(when)
            def _(units=units):
                finish(s, units)
        return 0

    lax.fori_loop(0, slots, second, 0)
    drain(0)
    drain(1)
    each_dead(lambda c: c.wait())


def per_device(latents, decoder_group, frames, conv_in, norm_gain, conv_mid, conv_up):
    groups, tiles = lax.axis_size("src"), lax.axis_size("tile")
    clips, slab, rows, packed = latents.shape
    lc, C = conv_in.shape[3:]
    width = packed // lc
    out_c = conv_up.shape[-1]
    slots = groups * CAP
    lat = latents.reshape(clips, slab, rows, width, lc).transpose(3, 0, 2, 1, 4).reshape(width, -1)
    group = decoder_group.reshape(-1)
    vmem = pl.BlockSpec(memory_space=pltpu.VMEM)
    smem = pl.BlockSpec(memory_space=pltpu.SMEM)
    hbm = pl.BlockSpec(memory_space=pltpu.HBM)
    taps = 2 * REACH + 1
    recv = pl.pallas_call(
        functools.partial(exchange_kernel, groups, tiles),
        out_shape=jax.ShapeDtypeStruct((2, taps, groups, width, 128), BF),
        in_specs=[smem, vmem],
        out_specs=vmem,
        scratch_shapes=[
            pltpu.VMEM((groups, width, 128), BF),
            pltpu.SemaphoreType.DMA((taps, groups)),
            pltpu.SemaphoreType.DMA((taps, groups)),
            pltpu.SemaphoreType.DMA((taps,)),
            pltpu.SemaphoreType.DMA((taps,)),
        ],
        compiler_params=pltpu.CompilerParams(
            collective_id=0, has_side_effects=True, vmem_limit_bytes=8 * 1024 * 1024
        ),
        cost_estimate=pl.CostEstimate(flops=40_000_000_000, bytes_accessed=40_000_000, transcendentals=0),
    )(group, lat)

    return pl.pallas_call(
        functools.partial(decode_kernel, groups, tiles),
        out_shape=jax.ShapeDtypeStruct((slots, slab, 2 * rows, 2 * width * out_c), BF),
        in_specs=[smem, smem, vmem, vmem, vmem, vmem, vmem],
        out_specs=hbm,
        scratch_shapes=[
            pltpu.SMEM((slots,), jnp.int32),
            pltpu.VMEM((2, 2 * C, 4 * out_c), BF),
            pltpu.VMEM((4 * out_c, C), BF),
            pltpu.VMEM((3, width, 4 * FR * lc * 2), BF),
            pltpu.VMEM((slots, FR, 6, width, C), BF),
            pltpu.VMEM((slots, FR, 4, width, C), BF),
            pltpu.VMEM((2, 4 * width, 3 * C), F32),
            pltpu.VMEM((2, 4, width, C), BF),
            pltpu.VMEM((2, C // 128, 4 * width, 128), F32),
            pltpu.VMEM((2, 2, 2 * rows, 2 * width * out_c), BF),
            pltpu.VMEM((2 * rows, 2 * width * out_c), BF),
            pltpu.SMEM((5,), jnp.int32),
            pltpu.SemaphoreType.DMA((slots, 2)),
            pltpu.SemaphoreType.DMA((2, 2)),
        ],
        compiler_params=pltpu.CompilerParams(vmem_limit_bytes=32 * 1024 * 1024),
    )(group, frames, recv, norm_gain, conv_in, conv_mid, conv_up.transpose(0, 1, 3, 2))


def solution(mesh):
    placed = (P("src", "tm", "tile", None), P(), P(), P(), P(), P(), P())
    return jax.shard_map(
        per_device,
        mesh=mesh,
        in_specs=placed,
        out_specs=P("src", "tm", "tile", None),
        check_vma=False,
    )
```

```python
import functools

import jax
import jax.numpy as jnp
from jax import lax
from jax.experimental import pallas as pl
from jax.experimental.pallas import tpu as pltpu
from jax.sharding import PartitionSpec as P

CAP = 2
FR = 4
REACH = 2
MESH = pl.DeviceIdType.MESH
BF = jnp.bfloat16
F32 = jnp.float32


def shift_down(x, first):
    return jnp.where(first, 0.0, pltpu.roll(x, 1, x.ndim - 2))


def shift_up(x, last):
    return jnp.where(last, 0.0, pltpu.roll(x, x.shape[-2] - 1, x.ndim - 2))


def exchange_kernel(
    groups, tiles, group_ref, lat_ref, mid_hbm, recv_ref, wide0_ref, wide1_ref, wide2_ref, wide3_ref, out_ref, mid_ref, send_sem, recv_sem, fwd_send, fwd_recv, mid_sem
):
    src, tm, tile = lax.axis_index("src"), lax.axis_index("tm"), lax.axis_index("tile")
    clips = 4

    def ok(d):
        return jnp.logical_and(tile + d >= 0, tile + d < tiles)

    mids = [pltpu.make_async_copy(mid_hbm.at[a], mid_ref.at[a], mid_sem.at[a]) for a in range(3)]
    for mid in mids:
        mid.start()

    partners = [(k, d) for d in (2, -2, 1, -1, 0) for k in (2, 1, 3, 0) if (k, d) != (0, 0)]

    barrier = pltpu.get_barrier_semaphore()
    for k, d in partners:
        @pl.when(ok(d))
        def _(k=k, d=d):
            pl.semaphore_signal(
                barrier, inc=1, device_id={"src": lax.rem(src + k, groups), "tile": tile + d}, device_id_type=MESH
            )
    pl.semaphore_signal(barrier, inc=1, device_id={"tm": 1 - tm}, device_id_type=MESH)

    blocks = []
    for i in range(clips):
        block = lat_ref[:, 128 * (i // 2) : 128 * (i // 2) + 128].astype(F32)
        blocks.append((block, pltpu.roll(block, 64, 1)))
    lane = lax.broadcasted_iota(jnp.int32, blocks[0][0].shape, 1)
    targets = [group_ref[src * clips + i] for i in range(clips)]
    ranks = []
    for i in range(clips):
        rank = jnp.int32(0)
        for e in range(i):
            rank = rank + jnp.where(targets[e] == targets[i], 1, 0)
        ranks.append(rank)
    for g in range(groups):
        parts = []
        for k in range(CAP):
            total = jnp.zeros(lane.shape, F32)
            for i in range(clips):
                mine = jnp.logical_and(targets[i] == g, ranks[i] == k)
                total = total + blocks[i][(i + k) % 2] * jnp.where(mine, 1.0, 0.0)
            parts.append(total)
        out_ref[g] = jnp.where(lane < 64, parts[0], parts[1]).astype(BF)

    for d in (-2, -1, 1, 2):
        @pl.when(jnp.logical_not(ok(d)))
        def _(d=d):
            recv_ref[tm, d + REACH] = jnp.zeros(recv_ref.shape[2:], BF)

    @pl.when(tm == 0)
    def _():
        recv_ref[1] = jnp.zeros(recv_ref.shape[1:], BF)

    recv_ref[tm, REACH, src] = out_ref[src]

    nd = jnp.int32(1)
    for d in (-2, -1, 1, 2):
        nd = nd + jnp.where(ok(d), 1, 0)
    pl.semaphore_wait(barrier, groups * nd)

    def copy(k, d):
        g = lax.rem(src + k, groups)
        return pltpu.make_async_remote_copy(
            src_ref=out_ref.at[g],
            dst_ref=recv_ref.at[tm, REACH - d, src],
            send_sem=send_sem.at[d + REACH, k],
            recv_sem=recv_sem.at[REACH - d, src],
            device_id={"src": g, "tile": tile + d},
            device_id_type=MESH,
        )

    for k, d in partners:
        @pl.when(ok(d))
        def _(k=k, d=d):
            copy(k, d).start()

    depth, step = mid_ref.shape[3], 32
    for a, mid in enumerate(mids):
        mid.wait()

        def turn(i, _, a=a):
            at = pl.ds(pl.multiple_of(i * step, step), step)
            for c in range(3):
                g0, g1, g2 = [mid_ref[a, b, c, at, :] for b in range(3)]
                even = 0.5 * (g0.astype(F32) + g2.astype(F32))
                odd = 0.5 * g1.astype(F32)
                lanes = slice(c * depth, (c + 1) * depth)
                wide0_ref[a, at, lanes] = g0
                wide1_ref[a, at, lanes] = (even + odd).astype(BF)
                wide2_ref[a, at, lanes] = (even - odd).astype(BF)
                wide3_ref[a, at, lanes] = g2
            return 0

        lax.fori_loop(0, depth // step, turn, 0)

    def forward(d):
        return pltpu.make_async_remote_copy(
            src_ref=recv_ref.at[0, d + REACH],
            dst_ref=recv_ref.at[0, d + REACH],
            send_sem=fwd_send.at[d + REACH],
            recv_sem=fwd_recv.at[d + REACH],
            device_id={"tm": 1 - tm},
            device_id_type=MESH,
        )

    for d in (0, 1, -1, 2, -2):
        for k in range(groups):
            if (k, d) == (0, 0):
                continue
            s = lax.rem(src + k, groups)

            @pl.when(ok(d))
            def _(d=d, s=s):
                pltpu.make_async_remote_copy(
                    src_ref=out_ref.at[0],
                    dst_ref=recv_ref.at[tm, d + REACH, s],
                    send_sem=send_sem.at[d + REACH, 0],
                    recv_sem=recv_sem.at[d + REACH, s],
                    device_id={"tm": 1 - tm},
                    device_id_type=MESH,
                ).wait_recv()

        @pl.when(tm == 0)
        def _(d=d):
            forward(d).start()

    for k, d in partners:
        @pl.when(ok(d))
        def _(k=k, d=d):
            copy(k, d).wait_send()

    for d in (0, 1, -1, 2, -2):
        @pl.when(tm == 0)
        def _(d=d):
            forward(d).wait_send()

        @pl.when(tm == 1)
        def _(d=d):
            forward(d).wait_recv()


def decode_kernel(
    groups,
    tiles,
    group_ref,
    frames_ref,
    recv_ref,
    gain_ref,
    cin_ref,
    wide0_ref,
    wide1_ref,
    wide2_ref,
    wide3_ref,
    cup_ref,
    out_hbm,
    count_ref,
    list_ref,
    up_ref,
    turn_ref,
    z_ref,
    act_ref,
    hid_ref,
    acc_ref,
    res_ref,
    y_ref,
    o_ref,
    zero_ref,
    used_ref,
    zero_sem,
    o_sem,
):
    src, tm, tile = lax.axis_index("src"), lax.axis_index("tm"), lax.axis_index("tile")
    clips, slots = 4, groups * CAP
    C = gain_ref.shape[-1]
    Wd = z_ref.shape[3]
    top, bottom = tile == 0, tile == tiles - 1

    for s in range(slots):
        count_ref[s] = 0
    for s in range(groups):
        seen = jnp.int32(0)
        for i in range(clips):
            hit = group_ref[s * clips + i] == src

            @pl.when(hit)
            def _(s=s, i=i, seen=seen):
                count_ref[s * CAP + jnp.minimum(seen, CAP - 1)] = frames_ref[s * clips + i]

            seen = seen + jnp.where(hit, 1, 0)

    zero_ref[...] = jnp.zeros(zero_ref.shape, BF)

    def clear(s, o):
        return pltpu.make_async_copy(zero_ref, out_hbm.at[s, o], zero_sem.at[s, o])

    def each_dead(go):
        def body(s, _):
            for o in range(2):
                @pl.when(2 * tm + o >= count_ref[s])
                def _():
                    go(clear(s, o))
            return 0
        lax.fori_loop(0, slots, body, 0)

    each_dead(lambda c: c.start())

    width = cup_ref.shape[-2]
    for p in range(2):
        for i in range(2):
            rows = ((0,), (1, 2)) if p == 0 else ((0, 1), (2,))
            k0, k1, k2 = [
                functools.reduce(jnp.add, [cup_ref[b, c].astype(F32) for b in rows[i]]) for c in range(3)
            ]
            for at, value in enumerate((k1 + k2, k0 + k1, k0, k2)):
                turn_ref[at * width : (at + 1) * width, :] = value.astype(BF)
            up_ref[p, i * C : (i + 1) * C, :] = turn_ref[...].T

    lane = lax.broadcasted_iota(jnp.int32, (Wd, 128), 1)
    spot = lax.broadcasted_iota(jnp.int32, (Wd, 1), 0)
    gain = 0.5 * gain_ref[...].reshape(1, C)
    row = lax.broadcasted_iota(jnp.int32, (3 * Wd, 1), 0)
    inside = jnp.logical_not(
        jnp.logical_or(jnp.logical_and(top, row < Wd), jnp.logical_and(bottom, row >= 2 * Wd))
    )
    nothing = jnp.zeros((16, C), BF)

    def band(f):
        rows = []
        for h in range(f // 2 + 1):
            for c in range(3):
                for row in range(4):
                    for t in (2 * h, 2 * h + 1):
                        a = t - f + 2
                        rows.append(
                            jnp.concatenate(
                                [
                                    cin_ref[a, row - q, c] if 0 <= a <= 2 and 0 <= row - q <= 2 else nothing
                                    for q in range(2)
                                ],
                                axis=1,
                            )
                        )
        return jnp.concatenate(rows, axis=0)

    def hidden(s, frames):
        lhs = jnp.concatenate(
            [
                jnp.concatenate(
                    [z_ref[h, c, j] for h in range(frames[0] // 2 + 1) for c in range(3)], axis=1
                )
                for j in range(3)
            ],
            axis=0,
        )
        all_h = jnp.dot(lhs, jnp.concatenate([band(f) for f in frames], axis=1), preferred_element_type=F32)
        for e, f in enumerate(frames):
            h = all_h[:, e * 2 * C : (e + 1) * 2 * C]
            acts = {}
            for q in range(2):
                hf = h[:, q * C : (q + 1) * C]
                ms = jnp.sum(hf * hf, axis=-1, keepdims=True) * (1.0 / C)
                x = hf * jnp.where(inside, lax.rsqrt(ms + 1e-06), 0.0) * gain
                act = x + x * jnp.tanh(x)
                for j in range(3):
                    r = 2 * j + q
                    acts[r] = act[j * Wd : (j + 1) * Wd]
                    if 1 <= r <= 4:
                        hid_ref[s, f, (r - 1) % 2, (r - 1) // 2] = hf[j * Wd : (j + 1) * Wd].astype(BF)
            for i in range(2):
                d0, d1, d2, d3 = [acts[2 * i + e] for e in range(4)]
                for e, value in enumerate((d0 - d2, d1 + d2, d2 - d1, d1 - d3)):
                    act_ref[s, f, e, i] = value.astype(BF)

    def first(s, _):
        n = count_ref[s]
        need = jnp.where(tm == 0, jnp.minimum(n, 2), jnp.where(n >= 3, n, 0))

        @pl.when(need > 0)
        def _():
            sender, k = s // CAP, lax.rem(s, CAP)

            def gather(h):
                blocks = [recv_ref[h, d, sender].astype(F32) for d in range(2 * REACH + 1)]
                outer = [pltpu.roll(b, 96 - 64 * k, 1) for b in blocks]
                inner = [pltpu.roll(b, lax.rem(160 - 64 * k, 128), 1) for b in blocks[1:4]]
                for j in range(3):
                    z = jnp.where(lane < 32, outer[j], jnp.where(lane < 96, inner[j], outer[j + 2]))
                    z_ref[h, 0, j] = shift_down(z, spot == 0).astype(BF)
                    z_ref[h, 1, j] = z.astype(BF)
                    z_ref[h, 2, j] = shift_up(z, spot == Wd - 1).astype(BF)

            gather(0)

            @pl.when(tm == 1)
            def _():
                gather(1)

        for frames, when in (
            ((0,), need == 1),
            ((0, 1), need >= 2),
            ((2,), need == 3),
            ((2, 3), need == 4),
        ):
            @pl.when(when)
            def _(frames=frames):
                hidden(s, frames)
        return 0

    lax.fori_loop(0, slots, first, 0)

    spot2 = lax.broadcasted_iota(jnp.int32, (2, Wd, 1), 1)
    left = lax.broadcasted_iota(jnp.int32, (2, Wd, C), 2) < C // 2
    for e in range(5):
        used_ref[e] = 0

    def drain(buf):
        for e in range(2):
            @pl.when(used_ref[1 + 2 * buf + e] == 1)
            def _(e=e):
                pltpu.make_async_copy(o_ref.at[buf, e], out_hbm.at[0, 0], o_sem.at[buf, e]).wait()
                used_ref[1 + 2 * buf + e] = 0

    def finish(units, taps):
        count = len(units)
        M = 2 * Wd * count
        used = used_ref[0]
        buf = lax.rem(used, 2)
        for k in range(4):
            lhs = jnp.concatenate(
                [
                    jnp.concatenate(
                        [act_ref[s, 2 * tm + o + a - 2, k].reshape(2 * Wd, C) for a in range(3 - taps, 3)], axis=1
                    )
                    for s, o in units
                ],
                axis=0,
            )
            rhs = (wide0_ref, wide1_ref, wide2_ref, wide3_ref)[k][3 - taps :].reshape(taps * C, 3 * C)
            acc_ref[k, :M] = jnp.dot(lhs, rhs, preferred_element_type=F32)

        drain(buf)

        for e, (s, o) in enumerate(units):
            f = 2 * tm + o
            at = slice(e * 2 * Wd, (e + 1) * 2 * Wd)
            for q in range(2):
                def row(c):
                    lanes = slice(c * C, (c + 1) * C)
                    m = [acc_ref[k, at, lanes] for k in ((0, 1, 2), (1, 2, 3))[q]]
                    return (m[0] + m[1] + m[2] if q == 0 else m[0] - m[1] - m[2]).reshape(2, Wd, C)

                total = row(1) + hid_ref[s, f, q].astype(F32)
                total = total + shift_down(row(0), spot2 == 0)
                total = total + shift_up(row(2), spot2 == Wd - 1)
                for i in range(2):
                    part = total[i]
                    if (i, q) == (0, 0):
                        part = jnp.where(top, 0.0, part)
                    if (i, q) == (1, 1):
                        part = jnp.where(bottom, 0.0, part)
                    res_ref[e, 2 * i + q] = part.astype(BF)

        for p in range(2):
            lhs = jnp.concatenate(
                [
                    jnp.concatenate(
                        [res_ref[e, p : p + 2].reshape(2 * Wd, C), res_ref[e, p + 1 : p + 3].reshape(2 * Wd, C)],
                        axis=1,
                    )
                    for e in range(count)
                ],
                axis=0,
            )
            both = jnp.dot(lhs, up_ref[p], preferred_element_type=F32)
            for e in range(count):
                y = both[e * 2 * Wd : (e + 1) * 2 * Wd]
                still = y[:, :C].reshape(2, Wd, C)
                moved = y[:, C:].reshape(2, Wd, C)
                for v in range(C // 128):
                    at = slice(v * 128, v * 128 + 128)
                    part = moved[..., at]
                    if 2 * (v + 1) * 128 <= C:
                        part = shift_down(part, spot2 == 0)
                    elif 2 * v * 128 >= C:
                        part = shift_up(part, spot2 == Wd - 1)
                    else:
                        part = jnp.where(left[..., at], shift_down(part, spot2 == 0), shift_up(part, spot2 == Wd - 1))
                    part = part + still[..., at]
                    for h in range(2):
                        y_ref[e, v, pl.ds((2 * h + p) * Wd, Wd), :] = part[h]

        for e, (s, o) in enumerate(units):
            for w in range(Wd):
                for v in range(C // 128):
                    at = w * C + v * 128
                    o_ref[buf, e, :, at : at + 128] = y_ref[e, v, pl.ds(w, 4, stride=Wd), :].astype(BF)
            pltpu.make_async_copy(o_ref.at[buf, e], out_hbm.at[s, o], o_sem.at[buf, e]).start()
            used_ref[1 + 2 * buf + e] = 1
        used_ref[0] = used + 1

    for kind in range(3):
        list_ref[kind, 2 * slots] = 0
    for s in range(slots):
        for o in range(2):
            kind = jnp.where(tm == 0, o, 2)

            @pl.when(2 * tm + o < count_ref[s])
            def _(s=s, o=o, kind=kind):
                at = list_ref[kind, 2 * slots]
                list_ref[kind, at] = 2 * s + o
                list_ref[kind, 2 * slots] = at + 1

    for kind in range(3):
        total = list_ref[kind, 2 * slots]

        def unit(i, kind=kind):
            u = list_ref[kind, i]
            return u // 2, lax.rem(u, 2)

        def second(i, _, kind=kind, unit=unit):
            finish((unit(2 * i), unit(2 * i + 1)), kind + 1)
            return 0

        lax.fori_loop(0, total // 2, second, 0)

        @pl.when(lax.rem(total, 2) == 1)
        def _(kind=kind, unit=unit, total=total):
            finish((unit(total - 1),), kind + 1)

    drain(0)
    drain(1)
    each_dead(lambda c: c.wait())


def per_device(latents, decoder_group, frames, conv_in, norm_gain, conv_mid, conv_up):
    groups, tiles = lax.axis_size("src"), lax.axis_size("tile")
    clips, slab, rows, packed = latents.shape
    lc, C = conv_in.shape[3:]
    width = packed // lc
    out_c = conv_up.shape[-1]
    slots = groups * CAP
    lat = latents.reshape(clips, slab, rows, width, lc).transpose(3, 0, 2, 1, 4).reshape(width, -1)
    group = decoder_group.reshape(-1)
    vmem = pl.BlockSpec(memory_space=pltpu.VMEM)
    smem = pl.BlockSpec(memory_space=pltpu.SMEM)
    hbm = pl.BlockSpec(memory_space=pltpu.HBM)
    taps = 2 * REACH + 1
    recv, *wide = pl.pallas_call(
        functools.partial(exchange_kernel, groups, tiles),
        out_shape=(
            jax.ShapeDtypeStruct((2, taps, groups, width, 128), BF),
            *[jax.ShapeDtypeStruct((3, C, 3 * C), BF)] * 4,
        ),
        in_specs=[smem, vmem, hbm],
        out_specs=(vmem,) * 5,
        scratch_shapes=[
            pltpu.VMEM((groups, width, 128), BF),
            pltpu.VMEM(conv_mid.shape, BF),
            pltpu.SemaphoreType.DMA((taps, groups)),
            pltpu.SemaphoreType.DMA((taps, groups)),
            pltpu.SemaphoreType.DMA((taps,)),
            pltpu.SemaphoreType.DMA((taps,)),
            pltpu.SemaphoreType.DMA((3,)),
        ],
        compiler_params=pltpu.CompilerParams(
            collective_id=0, has_side_effects=True, vmem_limit_bytes=38 * 1024 * 1024
        ),
        cost_estimate=pl.CostEstimate(flops=40_000_000_000, bytes_accessed=40_000_000, transcendentals=0),
    )(group, lat, conv_mid)

    return pl.pallas_call(
        functools.partial(decode_kernel, groups, tiles),
        out_shape=jax.ShapeDtypeStruct((slots, slab, 2 * rows, 2 * width * out_c), BF),
        in_specs=[smem, smem] + [vmem] * 8,
        out_specs=hbm,
        scratch_shapes=[
            pltpu.SMEM((slots,), jnp.int32),
            pltpu.SMEM((3, 2 * slots + 1), jnp.int32),
            pltpu.VMEM((2, 2 * C, 4 * out_c), BF),
            pltpu.VMEM((4 * out_c, C), BF),
            pltpu.VMEM((2, 3, 3, width, 128), BF),
            pltpu.VMEM((slots, FR, 4, 2, width, C), BF),
            pltpu.VMEM((slots, FR, 2, 2, width, C), BF),
            pltpu.VMEM((4, 4 * width, 3 * C), F32),
            pltpu.VMEM((2, 4, width, C), BF),
            pltpu.VMEM((2, C // 128, 4 * width, 128), F32),
            pltpu.VMEM((2, 2, 2 * rows, 2 * width * out_c), BF),
            pltpu.VMEM((2 * rows, 2 * width * out_c), BF),
            pltpu.SMEM((5,), jnp.int32),
            pltpu.SemaphoreType.DMA((slots, 2)),
            pltpu.SemaphoreType.DMA((2, 2)),
        ],
        compiler_params=pltpu.CompilerParams(vmem_limit_bytes=32 * 1024 * 1024),
    )(group, frames, recv, norm_gain, conv_in, *wide, conv_up.transpose(0, 1, 3, 2))


def solution(mesh):
    placed = (P("src", "tm", "tile", None), P(), P(), P(), P(), P(), P())
    return jax.shard_map(
        per_device,
        mesh=mesh,
        in_specs=placed,
        out_specs=P("src", "tm", "tile", None),
        check_vma=False,
    )
```

```python
import functools

import jax
import jax.numpy as jnp
from jax import lax
from jax.experimental import pallas as pl
from jax.experimental.pallas import tpu as pltpu
from jax.sharding import PartitionSpec as P

CAP = 2
FR = 4
REACH = 2
MESH = pl.DeviceIdType.MESH
BF = jnp.bfloat16
F32 = jnp.float32


def shift_down(x, first):
    return jnp.where(first, 0.0, pltpu.roll(x, 1, x.ndim - 2))


def shift_up(x, last):
    return jnp.where(last, 0.0, pltpu.roll(x, x.shape[-2] - 1, x.ndim - 2))


def exchange_kernel(
    groups, tiles, group_ref, lat_ref, mid_hbm, recv_ref, wide0_ref, wide1_ref, wide2_ref, wide3_ref, out_ref, mid_ref, send_sem, recv_sem, fwd_send, fwd_recv, mid_sem
):
    src, tm, tile = lax.axis_index("src"), lax.axis_index("tm"), lax.axis_index("tile")
    clips = 4

    def ok(d):
        return jnp.logical_and(tile + d >= 0, tile + d < tiles)

    mids = [pltpu.make_async_copy(mid_hbm.at[a], mid_ref.at[a], mid_sem.at[a]) for a in range(3)]
    for mid in mids:
        mid.start()

    partners = [(k, d) for k in (2, 1, 3, 0) for d in (2, -2, 1, -1, 0) if (k, d) != (0, 0)]

    barrier = pltpu.get_barrier_semaphore()
    for k, d in partners:
        @pl.when(ok(d))
        def _(k=k, d=d):
            pl.semaphore_signal(
                barrier, inc=1, device_id={"src": lax.rem(src + k, groups), "tile": tile + d}, device_id_type=MESH
            )
    pl.semaphore_signal(barrier, inc=1, device_id={"tm": 1 - tm}, device_id_type=MESH)

    blocks = []
    for i in range(clips):
        block = lat_ref[:, 128 * (i // 2) : 128 * (i // 2) + 128].astype(F32)
        blocks.append((block, pltpu.roll(block, 64, 1)))
    lane = lax.broadcasted_iota(jnp.int32, blocks[0][0].shape, 1)
    targets = [group_ref[src * clips + i] for i in range(clips)]
    ranks = []
    for i in range(clips):
        rank = jnp.int32(0)
        for e in range(i):
            rank = rank + jnp.where(targets[e] == targets[i], 1, 0)
        ranks.append(rank)
    for g in range(groups):
        parts = []
        for k in range(CAP):
            total = jnp.zeros(lane.shape, F32)
            for i in range(clips):
                mine = jnp.logical_and(targets[i] == g, ranks[i] == k)
                total = total + blocks[i][(i + k) % 2] * jnp.where(mine, 1.0, 0.0)
            parts.append(total)
        out_ref[g] = jnp.where(lane < 64, parts[0], parts[1]).astype(BF)

    for d in (-2, -1, 1, 2):
        @pl.when(jnp.logical_not(ok(d)))
        def _(d=d):
            recv_ref[tm, d + REACH] = jnp.zeros(recv_ref.shape[2:], BF)

    @pl.when(tm == 0)
    def _():
        recv_ref[1] = jnp.zeros(recv_ref.shape[1:], BF)

    recv_ref[tm, REACH, src] = out_ref[src]

    nd = jnp.int32(1)
    for d in (-2, -1, 1, 2):
        nd = nd + jnp.where(ok(d), 1, 0)
    pl.semaphore_wait(barrier, groups * nd)

    def copy(k, d):
        g = lax.rem(src + k, groups)
        return pltpu.make_async_remote_copy(
            src_ref=out_ref.at[g],
            dst_ref=recv_ref.at[tm, REACH - d, src],
            send_sem=send_sem.at[d + REACH, k],
            recv_sem=recv_sem.at[REACH - d, src],
            device_id={"src": g, "tile": tile + d},
            device_id_type=MESH,
        )

    for k, d in partners:
        @pl.when(ok(d))
        def _(k=k, d=d):
            copy(k, d).start()

    depth, step = mid_ref.shape[3], 32
    for a, mid in enumerate(mids):
        mid.wait()

        def turn(i, _, a=a):
            at = pl.ds(pl.multiple_of(i * step, step), step)
            for c in range(3):
                g0, g1, g2 = [mid_ref[a, b, c, at, :] for b in range(3)]
                even = 0.5 * (g0.astype(F32) + g2.astype(F32))
                odd = 0.5 * g1.astype(F32)
                lanes = slice(c * depth, (c + 1) * depth)
                wide0_ref[a, at, lanes] = g0
                wide1_ref[a, at, lanes] = (even + odd).astype(BF)
                wide2_ref[a, at, lanes] = (even - odd).astype(BF)
                wide3_ref[a, at, lanes] = g2
            return 0

        lax.fori_loop(0, depth // step, turn, 0)

    def forward(d):
        return pltpu.make_async_remote_copy(
            src_ref=recv_ref.at[0, d + REACH],
            dst_ref=recv_ref.at[0, d + REACH],
            send_sem=fwd_send.at[d + REACH],
            recv_sem=fwd_recv.at[d + REACH],
            device_id={"tm": 1 - tm},
            device_id_type=MESH,
        )

    for d in (1, -1, 0, 2, -2):
        for k in range(groups):
            if (k, d) == (0, 0):
                continue
            s = lax.rem(src + k, groups)

            @pl.when(ok(d))
            def _(d=d, s=s):
                pltpu.make_async_remote_copy(
                    src_ref=out_ref.at[0],
                    dst_ref=recv_ref.at[tm, d + REACH, s],
                    send_sem=send_sem.at[d + REACH, 0],
                    recv_sem=recv_sem.at[d + REACH, s],
                    device_id={"tm": 1 - tm},
                    device_id_type=MESH,
                ).wait_recv()

        @pl.when(tm == 0)
        def _(d=d):
            forward(d).start()

    for k, d in partners:
        @pl.when(ok(d))
        def _(k=k, d=d):
            copy(k, d).wait_send()

    for d in (0, 1, -1, 2, -2):
        @pl.when(tm == 0)
        def _(d=d):
            forward(d).wait_send()

        @pl.when(tm == 1)
        def _(d=d):
            forward(d).wait_recv()


def decode_kernel(
    groups,
    tiles,
    group_ref,
    frames_ref,
    recv_ref,
    gain_ref,
    cin_ref,
    wide0_ref,
    wide1_ref,
    wide2_ref,
    wide3_ref,
    cup_ref,
    out_hbm,
    count_ref,
    list_ref,
    up_ref,
    turn_ref,
    z_ref,
    act_ref,
    hid_ref,
    acc_ref,
    res_ref,
    y_ref,
    o_ref,
    zero_ref,
    used_ref,
    zero_sem,
    o_sem,
):
    src, tm, tile = lax.axis_index("src"), lax.axis_index("tm"), lax.axis_index("tile")
    clips, slots = 4, groups * CAP
    C = gain_ref.shape[-1]
    Wd = z_ref.shape[3]
    top, bottom = tile == 0, tile == tiles - 1

    for s in range(slots):
        count_ref[s] = 0
    for s in range(groups):
        seen = jnp.int32(0)
        for i in range(clips):
            hit = group_ref[s * clips + i] == src

            @pl.when(hit)
            def _(s=s, i=i, seen=seen):
                count_ref[s * CAP + jnp.minimum(seen, CAP - 1)] = frames_ref[s * clips + i]

            seen = seen + jnp.where(hit, 1, 0)

    zero_ref[...] = jnp.zeros(zero_ref.shape, BF)

    def clear(s, o):
        return pltpu.make_async_copy(zero_ref, out_hbm.at[s, o], zero_sem.at[s, o])

    def each_dead(go):
        def body(s, _):
            for o in range(2):
                @pl.when(2 * tm + o >= count_ref[s])
                def _():
                    go(clear(s, o))
            return 0
        lax.fori_loop(0, slots, body, 0)

    each_dead(lambda c: c.start())

    width = cup_ref.shape[-2]
    for p in range(2):
        for i in range(2):
            rows = ((0,), (1, 2)) if p == 0 else ((0, 1), (2,))
            k0, k1, k2 = [
                functools.reduce(jnp.add, [cup_ref[b, c].astype(F32) for b in rows[i]]) for c in range(3)
            ]
            for at, value in enumerate((k1 + k2, k0 + k1, k0, k2)):
                turn_ref[at * width : (at + 1) * width, :] = value.astype(BF)
            up_ref[p, i * C : (i + 1) * C, :] = turn_ref[...].T

    lane = lax.broadcasted_iota(jnp.int32, (Wd, 128), 1)
    spot = lax.broadcasted_iota(jnp.int32, (Wd, 1), 0)
    gain = 0.5 * gain_ref[...].reshape(1, C)
    row = lax.broadcasted_iota(jnp.int32, (3 * Wd, 1), 0)
    inside = jnp.logical_not(
        jnp.logical_or(jnp.logical_and(top, row < Wd), jnp.logical_and(bottom, row >= 2 * Wd))
    )
    nothing = jnp.zeros((16, C), BF)

    def band(f):
        rows = []
        for h in range(f // 2 + 1):
            for c in range(3):
                for row in range(4):
                    for t in (2 * h, 2 * h + 1):
                        a = t - f + 2
                        rows.append(
                            jnp.concatenate(
                                [
                                    cin_ref[a, row - q, c] if 0 <= a <= 2 and 0 <= row - q <= 2 else nothing
                                    for q in range(2)
                                ],
                                axis=1,
                            )
                        )
        return jnp.concatenate(rows, axis=0)

    def hidden(s, frames):
        lhs = jnp.concatenate(
            [
                jnp.concatenate(
                    [z_ref[h, c, j] for h in range(frames[0] // 2 + 1) for c in range(3)], axis=1
                )
                for j in range(3)
            ],
            axis=0,
        )
        all_h = jnp.dot(lhs, jnp.concatenate([band(f) for f in frames], axis=1), preferred_element_type=F32)
        for e, f in enumerate(frames):
            h = all_h[:, e * 2 * C : (e + 1) * 2 * C]
            acts = {}
            for q in range(2):
                hf = h[:, q * C : (q + 1) * C]
                ms = jnp.sum(hf * hf, axis=-1, keepdims=True) * (1.0 / C)
                x = hf * jnp.where(inside, lax.rsqrt(ms + 1e-06), 0.0) * gain
                act = x + x * jnp.tanh(x)
                for j in range(3):
                    r = 2 * j + q
                    acts[r] = act[j * Wd : (j + 1) * Wd]
                    if 1 <= r <= 4:
                        hid_ref[s, f, (r - 1) % 2, (r - 1) // 2] = hf[j * Wd : (j + 1) * Wd].astype(BF)
            for i in range(2):
                d0, d1, d2, d3 = [acts[2 * i + e] for e in range(4)]
                for e, value in enumerate((d0 - d2, d1 + d2, d2 - d1, d1 - d3)):
                    act_ref[s, f, e, i] = value.astype(BF)

    def first(s, _):
        n = count_ref[s]
        need = jnp.where(tm == 0, jnp.minimum(n, 2), jnp.where(n >= 3, n, 0))

        @pl.when(need > 0)
        def _():
            sender, k = s // CAP, lax.rem(s, CAP)

            def gather(h):
                blocks = [recv_ref[h, d, sender].astype(F32) for d in range(2 * REACH + 1)]
                outer = [pltpu.roll(b, 96 - 64 * k, 1) for b in blocks]
                inner = [pltpu.roll(b, lax.rem(160 - 64 * k, 128), 1) for b in blocks[1:4]]
                for j in range(3):
                    z = jnp.where(lane < 32, outer[j], jnp.where(lane < 96, inner[j], outer[j + 2]))
                    z_ref[h, 0, j] = shift_down(z, spot == 0).astype(BF)
                    z_ref[h, 1, j] = z.astype(BF)
                    z_ref[h, 2, j] = shift_up(z, spot == Wd - 1).astype(BF)

            gather(0)

            @pl.when(tm == 1)
            def _():
                gather(1)

        for frames, when in (
            ((0,), need == 1),
            ((0, 1), need >= 2),
            ((2,), need == 3),
            ((2, 3), need == 4),
        ):
            @pl.when(when)
            def _(frames=frames):
                hidden(s, frames)
        return 0

    lax.fori_loop(0, slots, first, 0)

    spot2 = lax.broadcasted_iota(jnp.int32, (2, Wd, 1), 1)
    left = lax.broadcasted_iota(jnp.int32, (2, Wd, C), 2) < C // 2
    for e in range(7):
        used_ref[e] = 0

    def drain(buf):
        for e in range(3):
            @pl.when(used_ref[1 + 3 * buf + e] == 1)
            def _(e=e):
                pltpu.make_async_copy(o_ref.at[buf, e], out_hbm.at[0, 0], o_sem.at[buf, e]).wait()
                used_ref[1 + 3 * buf + e] = 0

    def finish(units, taps):
        count = len(units)
        M = 2 * Wd * count
        used = used_ref[0]
        buf = lax.rem(used, 2)
        for k in range(4):
            lhs = jnp.concatenate(
                [
                    jnp.concatenate(
                        [act_ref[s, 2 * tm + o + a - 2, k].reshape(2 * Wd, C) for a in range(3 - taps, 3)], axis=1
                    )
                    for s, o in units
                ],
                axis=0,
            )
            rhs = (wide0_ref, wide1_ref, wide2_ref, wide3_ref)[k][3 - taps :].reshape(taps * C, 3 * C)
            acc_ref[k, :M] = jnp.dot(lhs, rhs, preferred_element_type=F32)

        drain(buf)

        for e, (s, o) in enumerate(units):
            f = 2 * tm + o
            at = slice(e * 2 * Wd, (e + 1) * 2 * Wd)
            for q in range(2):
                def row(c):
                    lanes = slice(c * C, (c + 1) * C)
                    m = [acc_ref[k, at, lanes] for k in ((0, 1, 2), (1, 2, 3))[q]]
                    return (m[0] + m[1] + m[2] if q == 0 else m[0] - m[1] - m[2]).reshape(2, Wd, C)

                total = row(1) + hid_ref[s, f, q].astype(F32)
                total = total + shift_down(row(0), spot2 == 0)
                total = total + shift_up(row(2), spot2 == Wd - 1)
                for i in range(2):
                    part = total[i]
                    if (i, q) == (0, 0):
                        part = jnp.where(top, 0.0, part)
                    if (i, q) == (1, 1):
                        part = jnp.where(bottom, 0.0, part)
                    res_ref[e, 2 * i + q] = part.astype(BF)

        for p in range(2):
            lhs = jnp.concatenate(
                [
                    jnp.concatenate(
                        [res_ref[e, p : p + 2].reshape(2 * Wd, C), res_ref[e, p + 1 : p + 3].reshape(2 * Wd, C)],
                        axis=1,
                    )
                    for e in range(count)
                ],
                axis=0,
            )
            both = jnp.dot(lhs, up_ref[p], preferred_element_type=F32)
            for e in range(count):
                y = both[e * 2 * Wd : (e + 1) * 2 * Wd]
                still = y[:, :C].reshape(2, Wd, C)
                moved = y[:, C:].reshape(2, Wd, C)
                for v in range(C // 128):
                    at = slice(v * 128, v * 128 + 128)
                    part = moved[..., at]
                    if 2 * (v + 1) * 128 <= C:
                        part = shift_down(part, spot2 == 0)
                    elif 2 * v * 128 >= C:
                        part = shift_up(part, spot2 == Wd - 1)
                    else:
                        part = jnp.where(left[..., at], shift_down(part, spot2 == 0), shift_up(part, spot2 == Wd - 1))
                    part = part + still[..., at]
                    for h in range(2):
                        y_ref[e, v, pl.ds((2 * h + p) * Wd, Wd), :] = part[h]

        for e, (s, o) in enumerate(units):
            for w in range(Wd):
                for v in range(C // 128):
                    at = w * C + v * 128
                    o_ref[buf, e, :, at : at + 128] = y_ref[e, v, pl.ds(w, 4, stride=Wd), :].astype(BF)
            pltpu.make_async_copy(o_ref.at[buf, e], out_hbm.at[s, o], o_sem.at[buf, e]).start()
            used_ref[1 + 3 * buf + e] = 1
        used_ref[0] = used + 1

    for kind in range(3):
        list_ref[kind, 2 * slots] = 0
    for s in range(slots):
        for o in range(2):
            kind = jnp.where(tm == 0, o, 2)

            @pl.when(2 * tm + o < count_ref[s])
            def _(s=s, o=o, kind=kind):
                at = list_ref[kind, 2 * slots]
                list_ref[kind, at] = 2 * s + o
                list_ref[kind, 2 * slots] = at + 1

    for kind in range(3):
        total = list_ref[kind, 2 * slots]

        def unit(i, kind=kind):
            u = list_ref[kind, i]
            return u // 2, lax.rem(u, 2)

        rest = lax.rem(total, 3)
        twos = jnp.where(rest == 0, 0, jnp.where(rest == 2, 1, jnp.where(total == 1, 0, 2)))
        threes = (total - 2 * twos) // 3

        def by_three(i, _, kind=kind, unit=unit):
            finish((unit(3 * i), unit(3 * i + 1), unit(3 * i + 2)), kind + 1)
            return 0

        def by_two(i, _, kind=kind, unit=unit, threes=threes):
            finish((unit(3 * threes + 2 * i), unit(3 * threes + 2 * i + 1)), kind + 1)
            return 0

        lax.fori_loop(0, threes, by_three, 0)
        lax.fori_loop(0, twos, by_two, 0)

        @pl.when(total == 1)
        def _(kind=kind, unit=unit):
            finish((unit(0),), kind + 1)

    drain(0)
    drain(1)
    each_dead(lambda c: c.wait())


def per_device(latents, decoder_group, frames, conv_in, norm_gain, conv_mid, conv_up):
    groups, tiles = lax.axis_size("src"), lax.axis_size("tile")
    clips, slab, rows, packed = latents.shape
    lc, C = conv_in.shape[3:]
    width = packed // lc
    out_c = conv_up.shape[-1]
    slots = groups * CAP
    lat = latents.reshape(clips, slab, rows, width, lc).transpose(3, 0, 2, 1, 4).reshape(width, -1)
    group = decoder_group.reshape(-1)
    vmem = pl.BlockSpec(memory_space=pltpu.VMEM)
    smem = pl.BlockSpec(memory_space=pltpu.SMEM)
    hbm = pl.BlockSpec(memory_space=pltpu.HBM)
    taps = 2 * REACH + 1
    recv, *wide = pl.pallas_call(
        functools.partial(exchange_kernel, groups, tiles),
        out_shape=(
            jax.ShapeDtypeStruct((2, taps, groups, width, 128), BF),
            *[jax.ShapeDtypeStruct((3, C, 3 * C), BF)] * 4,
        ),
        in_specs=[smem, vmem, hbm],
        out_specs=(vmem,) * 5,
        scratch_shapes=[
            pltpu.VMEM((groups, width, 128), BF),
            pltpu.VMEM(conv_mid.shape, BF),
            pltpu.SemaphoreType.DMA((taps, groups)),
            pltpu.SemaphoreType.DMA((taps, groups)),
            pltpu.SemaphoreType.DMA((taps,)),
            pltpu.SemaphoreType.DMA((taps,)),
            pltpu.SemaphoreType.DMA((3,)),
        ],
        compiler_params=pltpu.CompilerParams(
            collective_id=0, has_side_effects=True, vmem_limit_bytes=38 * 1024 * 1024
        ),
        cost_estimate=pl.CostEstimate(flops=40_000_000_000, bytes_accessed=40_000_000, transcendentals=0),
    )(group, lat, conv_mid)

    return pl.pallas_call(
        functools.partial(decode_kernel, groups, tiles),
        out_shape=jax.ShapeDtypeStruct((slots, slab, 2 * rows, 2 * width * out_c), BF),
        in_specs=[smem, smem] + [vmem] * 8,
        out_specs=hbm,
        scratch_shapes=[
            pltpu.SMEM((slots,), jnp.int32),
            pltpu.SMEM((3, 2 * slots + 1), jnp.int32),
            pltpu.VMEM((2, 2 * C, 4 * out_c), BF),
            pltpu.VMEM((4 * out_c, C), BF),
            pltpu.VMEM((2, 3, 3, width, 128), BF),
            pltpu.VMEM((slots, FR, 4, 2, width, C), BF),
            pltpu.VMEM((slots, FR, 2, 2, width, C), BF),
            pltpu.VMEM((4, 6 * width, 3 * C), F32),
            pltpu.VMEM((3, 4, width, C), BF),
            pltpu.VMEM((3, C // 128, 4 * width, 128), F32),
            pltpu.VMEM((2, 3, 2 * rows, 2 * width * out_c), BF),
            pltpu.VMEM((2 * rows, 2 * width * out_c), BF),
            pltpu.SMEM((7,), jnp.int32),
            pltpu.SemaphoreType.DMA((slots, 2)),
            pltpu.SemaphoreType.DMA((2, 3)),
        ],
        compiler_params=pltpu.CompilerParams(vmem_limit_bytes=32 * 1024 * 1024),
    )(group, frames, recv, norm_gain, conv_in, *wide, conv_up.transpose(0, 1, 3, 2))


def solution(mesh):
    placed = (P("src", "tm", "tile", None), P(), P(), P(), P(), P(), P())
    return jax.shard_map(
        per_device,
        mesh=mesh,
        in_specs=placed,
        out_specs=P("src", "tm", "tile", None),
        check_vma=False,
    )
```

```python
import functools

import jax
import jax.numpy as jnp
from jax import lax
from jax.experimental import pallas as pl
from jax.experimental.pallas import tpu as pltpu
from jax.sharding import PartitionSpec as P

CAP = 2
FR = 4
REACH = 2
MESH = pl.DeviceIdType.MESH
BF = jnp.bfloat16
F32 = jnp.float32


def shift_down(x, first):
    return jnp.where(first, 0.0, pltpu.roll(x, 1, x.ndim - 2))


def shift_up(x, last):
    return jnp.where(last, 0.0, pltpu.roll(x, x.shape[-2] - 1, x.ndim - 2))


def exchange_kernel(
    groups, tiles, group_ref, lat_ref, mid_hbm, recv_ref, wide0_ref, wide1_ref, wide2_ref, wide3_ref, out_ref, mid_ref, send_sem, recv_sem, fwd_send, fwd_recv, mid_sem
):
    src, tm, tile = lax.axis_index("src"), lax.axis_index("tm"), lax.axis_index("tile")
    clips = 4

    def ok(d):
        return jnp.logical_and(tile + d >= 0, tile + d < tiles)

    mids = [pltpu.make_async_copy(mid_hbm.at[a], mid_ref.at[a], mid_sem.at[a]) for a in range(3)]
    for mid in mids:
        mid.start()

    partners = [(k, d) for k in (2, 1, 3, 0) for d in (2, -2, 1, -1, 0) if (k, d) != (0, 0)]

    barrier = pltpu.get_barrier_semaphore()
    for k, d in partners:
        @pl.when(ok(d))
        def _(k=k, d=d):
            pl.semaphore_signal(
                barrier, inc=1, device_id={"src": lax.rem(src + k, groups), "tile": tile + d}, device_id_type=MESH
            )
    pl.semaphore_signal(barrier, inc=1, device_id={"tm": 1 - tm}, device_id_type=MESH)

    blocks = []
    for i in range(clips):
        block = lat_ref[:, 128 * (i // 2) : 128 * (i // 2) + 128].astype(F32)
        blocks.append((block, pltpu.roll(block, 64, 1)))
    lane = lax.broadcasted_iota(jnp.int32, blocks[0][0].shape, 1)
    targets = [group_ref[src * clips + i] for i in range(clips)]
    ranks = []
    for i in range(clips):
        rank = jnp.int32(0)
        for e in range(i):
            rank = rank + jnp.where(targets[e] == targets[i], 1, 0)
        ranks.append(rank)
    for g in range(groups):
        parts = []
        for k in range(CAP):
            total = jnp.zeros(lane.shape, F32)
            for i in range(clips):
                mine = jnp.logical_and(targets[i] == g, ranks[i] == k)
                total = total + blocks[i][(i + k) % 2] * jnp.where(mine, 1.0, 0.0)
            parts.append(total)
        out_ref[g] = jnp.where(lane < 64, parts[0], parts[1]).astype(BF)

    for d in (-2, -1, 1, 2):
        @pl.when(jnp.logical_not(ok(d)))
        def _(d=d):
            recv_ref[tm, d + REACH] = jnp.zeros(recv_ref.shape[2:], BF)

    @pl.when(tm == 0)
    def _():
        recv_ref[1] = jnp.zeros(recv_ref.shape[1:], BF)

    recv_ref[tm, REACH, src] = out_ref[src]

    nd = jnp.int32(1)
    for d in (-2, -1, 1, 2):
        nd = nd + jnp.where(ok(d), 1, 0)
    pl.semaphore_wait(barrier, groups * nd)

    def copy(k, d):
        g = lax.rem(src + k, groups)
        return pltpu.make_async_remote_copy(
            src_ref=out_ref.at[g],
            dst_ref=recv_ref.at[tm, REACH - d, src],
            send_sem=send_sem.at[d + REACH, k],
            recv_sem=recv_sem.at[REACH - d, src],
            device_id={"src": g, "tile": tile + d},
            device_id_type=MESH,
        )

    for k, d in partners:
        @pl.when(ok(d))
        def _(k=k, d=d):
            copy(k, d).start()

    depth, step = mid_ref.shape[3], 32
    for a, mid in enumerate(mids):
        mid.wait()

        def turn(i, _, a=a):
            at = pl.ds(pl.multiple_of(i * step, step), step)
            for c in range(3):
                g0, g1, g2 = [mid_ref[a, b, c, at, :] for b in range(3)]
                even = 0.5 * (g0.astype(F32) + g2.astype(F32))
                odd = 0.5 * g1.astype(F32)
                lanes = slice(c * depth, (c + 1) * depth)
                wide0_ref[a, at, lanes] = g0
                wide1_ref[a, at, lanes] = (even + odd).astype(BF)
                wide2_ref[a, at, lanes] = (even - odd).astype(BF)
                wide3_ref[a, at, lanes] = g2
            return 0

        lax.fori_loop(0, depth // step, turn, 0)

    def forward(d):
        return pltpu.make_async_remote_copy(
            src_ref=recv_ref.at[0, d + REACH],
            dst_ref=recv_ref.at[0, d + REACH],
            send_sem=fwd_send.at[d + REACH],
            recv_sem=fwd_recv.at[d + REACH],
            device_id={"tm": 1 - tm},
            device_id_type=MESH,
        )

    for d in (1, -1, 0, 2, -2):
        for k in range(groups):
            if (k, d) == (0, 0):
                continue
            s = lax.rem(src + k, groups)

            @pl.when(ok(d))
            def _(d=d, s=s):
                pltpu.make_async_remote_copy(
                    src_ref=out_ref.at[0],
                    dst_ref=recv_ref.at[tm, d + REACH, s],
                    send_sem=send_sem.at[d + REACH, 0],
                    recv_sem=recv_sem.at[d + REACH, s],
                    device_id={"tm": 1 - tm},
                    device_id_type=MESH,
                ).wait_recv()

        @pl.when(tm == 0)
        def _(d=d):
            forward(d).start()

    for k, d in partners:
        @pl.when(ok(d))
        def _(k=k, d=d):
            copy(k, d).wait_send()

    for d in (0, 1, -1, 2, -2):
        @pl.when(tm == 0)
        def _(d=d):
            forward(d).wait_send()

        @pl.when(tm == 1)
        def _(d=d):
            forward(d).wait_recv()


def decode_kernel(
    groups,
    tiles,
    group_ref,
    frames_ref,
    recv_ref,
    gain_ref,
    cin_ref,
    wide0_ref,
    wide1_ref,
    wide2_ref,
    wide3_ref,
    cup_ref,
    out_hbm,
    count_ref,
    list_ref,
    up_ref,
    turn_ref,
    z_ref,
    act_ref,
    hid_ref,
    acc_ref,
    res_ref,
    y_ref,
    o_ref,
    zero_ref,
    used_ref,
    zero_sem,
    o_sem,
):
    src, tm, tile = lax.axis_index("src"), lax.axis_index("tm"), lax.axis_index("tile")
    clips, slots = 4, groups * CAP
    C = gain_ref.shape[-1]
    Wd = z_ref.shape[3]
    top, bottom = tile == 0, tile == tiles - 1

    for s in range(slots):
        count_ref[s] = 0
    for s in range(groups):
        seen = jnp.int32(0)
        for i in range(clips):
            hit = group_ref[s * clips + i] == src

            @pl.when(hit)
            def _(s=s, i=i, seen=seen):
                count_ref[s * CAP + jnp.minimum(seen, CAP - 1)] = frames_ref[s * clips + i]

            seen = seen + jnp.where(hit, 1, 0)

    zero_ref[...] = jnp.zeros(zero_ref.shape, BF)

    def clear(s, o):
        return pltpu.make_async_copy(zero_ref, out_hbm.at[s, o], zero_sem.at[s, o])

    def each_dead(go):
        def body(s, _):
            for o in range(2):
                @pl.when(2 * tm + o >= count_ref[s])
                def _():
                    go(clear(s, o))
            return 0
        lax.fori_loop(0, slots, body, 0)

    each_dead(lambda c: c.start())

    width = cup_ref.shape[-2]
    for p in range(2):
        for i in range(2):
            rows = ((0,), (1, 2)) if p == 0 else ((0, 1), (2,))
            k0, k1, k2 = [
                functools.reduce(jnp.add, [cup_ref[b, c].astype(F32) for b in rows[i]]) for c in range(3)
            ]
            for at, value in enumerate((k1 + k2, k0 + k1, k0, k2)):
                turn_ref[at * width : (at + 1) * width, :] = value.astype(BF)
            up_ref[p, i * C : (i + 1) * C, :] = turn_ref[...].T

    lane = lax.broadcasted_iota(jnp.int32, (Wd, 128), 1)
    spot = lax.broadcasted_iota(jnp.int32, (Wd, 1), 0)
    gain = 0.5 * gain_ref[...].reshape(1, C)
    row = lax.broadcasted_iota(jnp.int32, (3 * Wd, 1), 0)
    inside = jnp.logical_not(
        jnp.logical_or(jnp.logical_and(top, row < Wd), jnp.logical_and(bottom, row >= 2 * Wd))
    )
    nothing = jnp.zeros((16, C), BF)

    def band(f):
        rows = []
        for h in range(f // 2 + 1):
            for c in range(3):
                for row in range(4):
                    for t in (2 * h, 2 * h + 1):
                        a = t - f + 2
                        rows.append(
                            jnp.concatenate(
                                [
                                    cin_ref[a, row - q, c] if 0 <= a <= 2 and 0 <= row - q <= 2 else nothing
                                    for q in range(2)
                                ],
                                axis=1,
                            )
                        )
        return jnp.concatenate(rows, axis=0)

    def hidden(s, frames):
        lhs = jnp.concatenate(
            [
                jnp.concatenate(
                    [z_ref[h, c, j] for h in range(frames[0] // 2 + 1) for c in range(3)], axis=1
                )
                for j in range(3)
            ],
            axis=0,
        )
        all_h = jnp.dot(lhs, jnp.concatenate([band(f) for f in frames], axis=1), preferred_element_type=F32)
        for e, f in enumerate(frames):
            h = all_h[:, e * 2 * C : (e + 1) * 2 * C]
            acts = {}
            for q in range(2):
                hf = h[:, q * C : (q + 1) * C]
                ms = jnp.sum(hf * hf, axis=-1, keepdims=True) * (1.0 / C)
                x = hf * jnp.where(inside, lax.rsqrt(ms + 1e-06), 0.0) * gain
                act = x + x * jnp.tanh(x)
                for j in range(3):
                    r = 2 * j + q
                    acts[r] = act[j * Wd : (j + 1) * Wd]
                    if 1 <= r <= 4:
                        hid_ref[s, f, (r - 1) % 2, (r - 1) // 2] = hf[j * Wd : (j + 1) * Wd].astype(BF)
            for i in range(2):
                d0, d1, d2, d3 = [acts[2 * i + e] for e in range(4)]
                for e, value in enumerate((d0 - d2, d1 + d2, d2 - d1, d1 - d3)):
                    act_ref[s, f, e, i] = value.astype(BF)

    def first(s, _):
        n = count_ref[s]
        need = jnp.where(tm == 0, jnp.minimum(n, 2), jnp.where(n >= 3, n, 0))

        @pl.when(need > 0)
        def _():
            sender, k = s // CAP, lax.rem(s, CAP)

            def gather(h):
                blocks = [recv_ref[h, d, sender].astype(F32) for d in range(2 * REACH + 1)]
                outer = [pltpu.roll(b, 96 - 64 * k, 1) for b in blocks]
                inner = [pltpu.roll(b, lax.rem(160 - 64 * k, 128), 1) for b in blocks[1:4]]
                for j in range(3):
                    z = jnp.where(lane < 32, outer[j], jnp.where(lane < 96, inner[j], outer[j + 2]))
                    z_ref[h, 0, j] = shift_down(z, spot == 0).astype(BF)
                    z_ref[h, 1, j] = z.astype(BF)
                    z_ref[h, 2, j] = shift_up(z, spot == Wd - 1).astype(BF)

            gather(0)

            @pl.when(tm == 1)
            def _():
                gather(1)

        for frames, when in (
            ((0,), need == 1),
            ((0, 1), need >= 2),
            ((2,), need == 3),
            ((2, 3), need == 4),
        ):
            @pl.when(when)
            def _(frames=frames):
                hidden(s, frames)
        return 0

    lax.fori_loop(0, slots, first, 0)

    spot2 = lax.broadcasted_iota(jnp.int32, (2, Wd, 1), 1)
    left = lax.broadcasted_iota(jnp.int32, (2, Wd, C), 2) < C // 2
    for e in range(7):
        used_ref[e] = 0

    def drain(buf):
        for e in range(3):
            @pl.when(used_ref[1 + 3 * buf + e] == 1)
            def _(e=e):
                pltpu.make_async_copy(o_ref.at[buf, e], out_hbm.at[0, 0], o_sem.at[buf, e]).wait()
                used_ref[1 + 3 * buf + e] = 0

    def finish(units, taps):
        count = len(units)
        M = 2 * Wd * count
        used = used_ref[0]
        buf = lax.rem(used, 2)
        for k in range(4):
            lhs = jnp.concatenate(
                [
                    jnp.concatenate(
                        [act_ref[s, 2 * tm + o + a - 2, k].reshape(2 * Wd, C) for a in range(3 - taps, 3)], axis=1
                    )
                    for s, o in units
                ],
                axis=0,
            )
            rhs = (wide0_ref, wide1_ref, wide2_ref, wide3_ref)[k][3 - taps :].reshape(taps * C, 3 * C)
            acc_ref[k, :M] = jnp.dot(lhs, rhs, preferred_element_type=F32)

        drain(buf)

        for e, (s, o) in enumerate(units):
            f = 2 * tm + o
            at = slice(e * 2 * Wd, (e + 1) * 2 * Wd)
            for q in range(2):
                def row(c):
                    lanes = slice(c * C, (c + 1) * C)
                    m = [acc_ref[k, at, lanes] for k in ((0, 1, 2), (1, 2, 3))[q]]
                    return (m[0] + m[1] + m[2] if q == 0 else m[0] - m[1] - m[2]).reshape(2, Wd, C)

                total = row(1) + hid_ref[s, f, q].astype(F32)
                total = total + shift_down(row(0), spot2 == 0)
                total = total + shift_up(row(2), spot2 == Wd - 1)
                for i in range(2):
                    part = total[i]
                    if (i, q) == (0, 0):
                        part = jnp.where(top, 0.0, part)
                    if (i, q) == (1, 1):
                        part = jnp.where(bottom, 0.0, part)
                    res_ref[e, 2 * i + q] = part.astype(BF)

        for p in range(2):
            lhs = jnp.concatenate(
                [
                    jnp.concatenate(
                        [res_ref[e, p : p + 2].reshape(2 * Wd, C), res_ref[e, p + 1 : p + 3].reshape(2 * Wd, C)],
                        axis=1,
                    )
                    for e in range(count)
                ],
                axis=0,
            )
            both = jnp.dot(lhs, up_ref[p], preferred_element_type=F32)
            for e in range(count):
                y = both[e * 2 * Wd : (e + 1) * 2 * Wd]
                still = y[:, :C].reshape(2, Wd, C)
                moved = y[:, C:].reshape(2, Wd, C)
                for v in range(C // 128):
                    at = slice(v * 128, v * 128 + 128)
                    part = moved[..., at]
                    if 2 * (v + 1) * 128 <= C:
                        part = shift_down(part, spot2 == 0)
                    elif 2 * v * 128 >= C:
                        part = shift_up(part, spot2 == Wd - 1)
                    else:
                        part = jnp.where(left[..., at], shift_down(part, spot2 == 0), shift_up(part, spot2 == Wd - 1))
                    part = part + still[..., at]
                    for h in range(2):
                        y_ref[e, v, pl.ds((2 * h + p) * Wd, Wd), :] = part[h]

        for e, (s, o) in enumerate(units):
            for w in range(Wd):
                for v in range(C // 128):
                    at = w * C + v * 128
                    o_ref[buf, e, :, at : at + 128] = y_ref[e, v, pl.ds(w, 4, stride=Wd), :].astype(BF)
            pltpu.make_async_copy(o_ref.at[buf, e], out_hbm.at[s, o], o_sem.at[buf, e]).start()
            used_ref[1 + 3 * buf + e] = 1
        used_ref[0] = used + 1

    for kind in range(3):
        list_ref[kind, 2 * slots] = 0
    for s in range(slots):
        for o in range(2):
            kind = jnp.where(tm == 0, o, 2)

            @pl.when(2 * tm + o < count_ref[s])
            def _(s=s, o=o, kind=kind):
                at = list_ref[kind, 2 * slots]
                list_ref[kind, at] = 2 * s + o
                list_ref[kind, 2 * slots] = at + 1

    for kind in range(3):
        total = list_ref[kind, 2 * slots]

        def unit(i, kind=kind):
            u = list_ref[kind, i]
            return u // 2, lax.rem(u, 2)

        rest = lax.rem(total, 3)
        twos = jnp.where(rest == 0, 0, jnp.where(rest == 2, 1, jnp.where(total == 1, 0, 2)))
        threes = (total - 2 * twos) // 3

        def by_three(i, _, kind=kind, unit=unit):
            finish((unit(3 * i), unit(3 * i + 1), unit(3 * i + 2)), kind + 1)
            return 0

        def by_two(i, _, kind=kind, unit=unit, threes=threes):
            finish((unit(3 * threes + 2 * i), unit(3 * threes + 2 * i + 1)), kind + 1)
            return 0

        lax.fori_loop(0, threes, by_three, 0)
        lax.fori_loop(0, twos, by_two, 0)

        @pl.when(total == 1)
        def _(kind=kind, unit=unit):
            finish((unit(0),), kind + 1)

    drain(0)
    drain(1)
    each_dead(lambda c: c.wait())


def per_device(latents, decoder_group, frames, conv_in, norm_gain, conv_mid, conv_up):
    groups, tiles = lax.axis_size("src"), lax.axis_size("tile")
    clips, slab, rows, packed = latents.shape
    lc, C = conv_in.shape[3:]
    width = packed // lc
    out_c = conv_up.shape[-1]
    slots = groups * CAP
    lat = latents.reshape(clips, slab, rows, width, lc).transpose(3, 0, 2, 1, 4).reshape(width, -1)
    group = decoder_group.reshape(-1)
    vmem = pl.BlockSpec(memory_space=pltpu.VMEM)
    smem = pl.BlockSpec(memory_space=pltpu.SMEM)
    hbm = pl.BlockSpec(memory_space=pltpu.HBM)
    taps = 2 * REACH + 1
    recv, *wide = pl.pallas_call(
        functools.partial(exchange_kernel, groups, tiles),
        out_shape=(
            jax.ShapeDtypeStruct((2, taps, groups, width, 128), BF),
            *[jax.ShapeDtypeStruct((3, C, 3 * C), BF)] * 4,
        ),
        in_specs=[smem, vmem, hbm],
        out_specs=(vmem,) * 5,
        scratch_shapes=[
            pltpu.VMEM((groups, width, 128), BF),
            pltpu.VMEM(conv_mid.shape, BF),
            pltpu.SemaphoreType.DMA((taps, groups)),
            pltpu.SemaphoreType.DMA((taps, groups)),
            pltpu.SemaphoreType.DMA((taps,)),
            pltpu.SemaphoreType.DMA((taps,)),
            pltpu.SemaphoreType.DMA((3,)),
        ],
        compiler_params=pltpu.CompilerParams(
            collective_id=0, has_side_effects=True, vmem_limit_bytes=38 * 1024 * 1024
        ),
        cost_estimate=pl.CostEstimate(flops=40_000_000_000, bytes_accessed=40_000_000, transcendentals=0),
    )(group, lat, conv_mid)

    return pl.pallas_call(
        functools.partial(decode_kernel, groups, tiles),
        out_shape=jax.ShapeDtypeStruct((slots, slab, 2 * rows, 2 * width * out_c), BF),
        in_specs=[smem, smem] + [vmem] * 8,
        out_specs=hbm,
        scratch_shapes=[
            pltpu.SMEM((slots,), jnp.int32),
            pltpu.SMEM((3, 2 * slots + 1), jnp.int32),
            pltpu.VMEM((2, 2 * C, 4 * out_c), BF),
            pltpu.VMEM((4 * out_c, C), BF),
            pltpu.VMEM((2, 3, 3, width, 128), BF),
            pltpu.VMEM((slots, FR, 4, 2, width, C), BF),
            pltpu.VMEM((slots, FR, 2, 2, width, C), BF),
            pltpu.VMEM((4, 6 * width, 3 * C), F32),
            pltpu.VMEM((3, 4, width, C), BF),
            pltpu.VMEM((3, C // 128, 8 * width, 128), F32),
            pltpu.VMEM((2, 3, 2 * rows, 2 * width * out_c), BF),
            pltpu.VMEM((2 * rows, 2 * width * out_c), BF),
            pltpu.SMEM((7,), jnp.int32),
            pltpu.SemaphoreType.DMA((slots, 2)),
            pltpu.SemaphoreType.DMA((2, 3)),
        ],
        compiler_params=pltpu.CompilerParams(vmem_limit_bytes=32 * 1024 * 1024),
    )(group, frames, recv, norm_gain, conv_in, *wide, conv_up.transpose(0, 1, 3, 2))


def solution(mesh):
    placed = (P("src", "tm", "tile", None), P(), P(), P(), P(), P(), P())
    return jax.shard_map(
        per_device,
        mesh=mesh,
        in_specs=placed,
        out_specs=P("src", "tm", "tile", None),
        check_vma=False,
    )
```
